32 devices in a mesh: wide: 8 (over z, x), narrow: 4 (over y, core).
Axes of the slice: x: 2, y: 2, z: 4, core: 2. Of those that a mesh axis runs over, the one named last changes fastest.
Arguments:
- tokens_in: bfloat16 [15680, 768], P(('wide', 'narrow')), may hold values from -6 to 6
- cotangent: float32 [15680, 768], P(('wide', 'narrow')), may hold values from -6 to 6
- norm1_gain: float32 [768], replicated, may hold values from 0.25 to 1.75
- norm1_shift: float32 [768], replicated, may hold values from -2 to 2
- w_query: bfloat16 [768, 768], P('wide', 'narrow'), may hold values from -0.3125 to 0.3125
- w_key: bfloat16 [768, 768], P('wide', 'narrow'), may hold values from -0.3125 to 0.3125
- w_value: bfloat16 [768, 768], P('wide', 'narrow'), may hold values from -0.21875 to 0.21875
- w_out: bfloat16 [768, 768], P('narrow', 'wide'), may hold values from -0.625 to 0.625
- norm2_gain: float32 [768], replicated, may hold values from 0.25 to 1.75
- norm2_shift: float32 [768], replicated, may hold values from -2 to 2
- w_up: bfloat16 [768, 3072], P('wide', 'narrow'), may hold values from -0.21875 to 0.21875
- up_bias: float32 [3072], P('narrow'), may hold values from -2.5 to 2.5
- w_down: bfloat16 [3072, 768], P('narrow', 'wide'), may hold values from -0.15625 to 0.15625
- down_bias: float32 [768], replicated, may hold values from -2.5 to 2.5
Outputs:
- layer_out: float32 [15680, 768], P(('wide', 'narrow'))
- grad_tokens: float32 [15680, 768], P(('wide', 'narrow'))
- grad_norm1_gain: float32 [768], replicated
- grad_norm1_shift: float32 [768], replicated
- grad_query: float32 [768, 768], P('wide', 'narrow')
- grad_key: float32 [768, 768], P('wide', 'narrow')
- grad_value: float32 [768, 768], P('wide', 'narrow')
- grad_out: float32 [768, 768], P('narrow', 'wide')
- grad_norm2_gain: float32 [768], replicated
- grad_norm2_shift: float32 [768], replicated
- grad_up: float32 [768, 3072], P('wide', 'narrow')
- grad_up_bias: float32 [3072], P('narrow')
- grad_down: float32 [3072, 768], P('narrow', 'wide')
- grad_down_bias: float32 [768], replicated
The draws below stay inside these ranges and needn't reach their ends.
All inputs are finite; a program needn't handle non-finite values.
Results may differ from the reference program's by a relative error of at most 0.013.
The reference program's roundings to bfloat16 on the way count: a program that leaves them out, or rounds other values in their place, can miss the bound.
Values may be sent and summed in bfloat16 or wider, within the bound.
No kernel may reach another device: no remote copies, remote signals or barrier semaphores. Data moves between devices by JAX's collectives and lax.ppermute only.
A program may use at most 192 MiB of HBM per device.

```python
import jax
import jax.numpy as jnp
from jax import lax

D = 768
HEADS = 12
HEAD_DIM = 64
FF = 3072
PATCHES = 196
F_DEV = 10
TOKENS = 15680
N_WIDE = 8


def spiked(values, rng, source, target, parts, factor):
    owner, partner = [(jnp.arange(values.shape[dim]) // (values.shape[dim] // parts)).reshape([-1 if axis == dim else 1 for axis in range(values.ndim)]) for dim in (source, target)]
    chosen = jax.random.permutation(rng, parts)[partner]
    strong = (owner == chosen) | (owner == (partner + parts // 2) % parts)
    return jnp.where(strong, factor * values, values)


def levels(stream_key, shape, cuts, low, high):
    level, own = 1.0, jax.random.fold_in(stream_key, 6)
    for axis_at, blocks in cuts:
        heights = jnp.exp(jax.random.uniform(jax.random.fold_in(own, axis_at), (blocks,), jnp.float32, low / len(cuts), high / len(cuts)))
        level = level * jnp.repeat(heights, shape[axis_at] // blocks).reshape([-1 if axis == axis_at else 1 for axis in range(len(shape))])
    return level


def scatter_about(rng, extent, width, bound, pieces=(), dtype=jnp.bfloat16):
    level = levels(rng, extent, pieces, -0.22, 0.18) if pieces else 1.0
    array = jax.random.normal(rng, extent, jnp.float32) * width * level
    return jnp.minimum(jnp.maximum(array, -bound), bound).astype(dtype)


def gaussian_with(key, shape, spread, limit, shards, heavy, held_as=jnp.bfloat16):
    entries = spread * jax.random.normal(key, shape, jnp.float32)
    if shards:
        entries = entries * levels(key, shape, shards, -0.22, 0.18)
    return jnp.clip(spiked(entries, jax.random.fold_in(key, 3), *heavy), -limit, limit).astype(held_as)


def setup_inputs(seed: int = 0) -> dict:
    streams_of = jax.random.split(jax.random.key(seed), 15)
    return {
        "tokens_in": scatter_about(streams_of[0], (TOKENS, D), 1.0, 6.0, ((0, 32),)),
        "cotangent": gaussian_with(streams_of[1], (TOKENS, D), 1.0, 6.0, ((0, 32),), (0, 1, 32, 2.75), jnp.float32),
        "norm1_gain": jnp.clip(1.0 + 0.15 * jax.random.normal(streams_of[2], (D,), jnp.float32), 0.25, 1.75),
        "norm1_shift": scatter_about(streams_of[3], (D,), 0.4, 2.0, (), jnp.float32),
        "w_query": scatter_about(streams_of[4], (D, D), (D // 2) ** -0.5, 0.3125, ((0, 8), (1, 4))),
        "w_key": scatter_about(streams_of[5], (D, D), (D // 2) ** -0.5, 0.3125, ((0, 8), (1, 4))),
        "w_value": scatter_about(streams_of[6], (D, D), D ** -0.5, 0.21875, ((0, 8), (1, 4))),
        "w_out": scatter_about(streams_of[7], (D, D), (D // 8) ** -0.5, 0.625, ((0, 4), (1, 8))),
        "norm2_gain": jnp.clip(1.0 + 0.15 * jax.random.normal(streams_of[8], (D,), jnp.float32), 0.25, 1.75),
        "norm2_shift": scatter_about(streams_of[9], (D,), 0.4, 2.0, (), jnp.float32),
        "w_up": scatter_about(streams_of[10], (D, FF), D ** -0.5, 0.21875, ((0, 8), (1, 4))),
        "up_bias": scatter_about(streams_of[11], (FF,), 0.5, 2.5, ((0, 4),), jnp.float32),
        "w_down": scatter_about(streams_of[12], (FF, D), (FF // 2) ** -0.5, 0.15625, ((0, 4), (1, 8))),
        "down_bias": scatter_about(streams_of[13], (D,), 0.5, 2.5, (), jnp.float32),
    }


@jax.custom_vjp
def low(v):
    return lax.optimization_barrier(v.astype(jnp.bfloat16)).astype(jnp.float32)

@jax.custom_vjp
def low_back(v):
    return v

def low_keep(v):
    return (low(v), None)

def low_pass(kept, grad):
    return (grad,)

def back_keep(v):
    return (v, None)

def back_low(kept, grad):
    return (low(grad),)
low.defvjp(low_keep, low_pass)
low_back.defvjp(back_keep, back_low)

def matmul(left, right):
    return jnp.dot(left, right, precision=lax.Precision.HIGHEST, preferred_element_type=jnp.float32)

def layer_norm(value, gain, shift):
    mean = lax.optimization_barrier(jnp.mean(value, axis=1, keepdims=True))
    var = lax.optimization_barrier(jnp.mean((value - mean) ** 2, axis=1, keepdims=True))
    return (value - mean) * lax.rsqrt(var + 1e-06) * gain + shift

def layer(x, gain_one, shift_one, wq, wk, wv, wo, gain_two, shift_two, wu, bias_up, wd, bias_down):
    frames = x.shape[0] // PATCHES
    scale = HEAD_DIM ** (-0.5)
    h_one = low(layer_norm(x, gain_one, shift_one))
    query = low_back(low(matmul(h_one, wq))).reshape(frames, PATCHES, HEADS, HEAD_DIM)
    key = low_back(low(matmul(h_one, wk))).reshape(frames, PATCHES, HEADS, HEAD_DIM)
    value = low_back(low(matmul(h_one, wv))).reshape(frames, PATCHES, HEADS, HEAD_DIM)
    scores = low_back(scale * jnp.einsum('fqhd,fkhd->fhqk', query, key, precision=lax.Precision.HIGHEST))
    probs = low(jax.nn.softmax(scores, axis=-1))
    mixed = jnp.einsum('fhqk,fkhd->fqhd', probs, value, precision=lax.Precision.HIGHEST).reshape(x.shape[0], D)
    mixed = low_back(low(mixed))
    y_mid = x + low_back(matmul(mixed, wo))
    h_two = low(layer_norm(y_mid, gain_two, shift_two))
    hidden = low_back(matmul(h_two, wu)) + bias_up
    active = low(jax.nn.gelu(hidden, approximate=False))
    return y_mid + low_back(matmul(active, wd)) + bias_down

def reference(tokens_in, cotangent, norm1_gain, norm1_shift, w_query, w_key, w_value, w_out, norm2_gain, norm2_shift, w_up, up_bias, w_down, down_bias):
    params = tuple((p.astype(jnp.float32) for p in (norm1_gain, norm1_shift, w_query, w_key, w_value, w_out, norm2_gain, norm2_shift, w_up, up_bias, w_down, down_bias)))
    group = F_DEV * PATCHES
    inputs = tokens_in.astype(jnp.float32).reshape(N_WIDE, group, D)
    cots = cotangent.astype(jnp.float32).reshape(N_WIDE, group, D)

    def step(totals, item):
        x_part, c_part = item
        result, pull = jax.vjp(layer, x_part, *params)
        grads = pull(c_part)
        totals = tuple((t + g for t, g in zip(totals, grads[1:])))
        return (totals, (result, grads[0]))
    start = tuple((jnp.zeros_like(p) for p in params))
    totals, (results, grad_x) = lax.scan(step, start, (inputs, cots))
    return (results.reshape(TOKENS, D), grad_x.reshape(TOKENS, D), totals[0], totals[1], totals[2], totals[3], totals[4], totals[5], totals[6], totals[7], totals[8], totals[9], totals[10], totals[11])
```

```python
import functools

import jax
import jax.numpy as jnp
from jax import lax
from jax.experimental import pallas as pl
from jax.experimental.pallas import tpu as pltpu
from jax.sharding import PartitionSpec as P

HEAD_DIM = 64
PATCHES = 196
EPS = 1e-06
D = 768
ROWS = 512
BLOCK = 208
FRAMES_AT = (0, 208)
HALF_AT = 400
HALF_ROWS = 112
HALF = PATCHES // 2
HALF_FIRST = 4
SCALE = HEAD_DIM ** (-0.5)
NEG = -1e30
BF = jnp.bfloat16
F32 = jnp.float32
PARAMS = pltpu.CompilerParams(vmem_limit_bytes=56 * 1024 * 1024)


def nn(left, right):
    return jnp.dot(left, right, preferred_element_type=F32)


def nt(left, right):
    return lax.dot_general(left, right, (((1,), (1,)), ((), ())), preferred_element_type=F32)


def tn(left, right):
    return lax.dot_general(left, right, (((0,), (0,)), ((), ())), preferred_element_type=F32)


def lanes_below(shape, bound):
    return lax.broadcasted_iota(jnp.int32, shape, 1) < bound


def ln_stats(value):
    mean = jnp.mean(value, axis=1, keepdims=True)
    centred = value - mean
    rstd = lax.rsqrt(jnp.mean(centred * centred, axis=1, keepdims=True) + EPS)
    return centred * rstd, rstd


def ln_back(grad, normed, rstd, gain):
    scaled = grad * gain
    first = jnp.mean(scaled, axis=1, keepdims=True)
    second = jnp.mean(scaled * normed, axis=1, keepdims=True)
    return rstd * (scaled - first - normed * second)


def split(block):
    return (
        block[:, 0:128],
        block[:, 128:256],
        block[:, 256:384],
        block[:, 512:640],
        block[:, 640:768],
    )


def masked_pair(pair, low):
    zero = jnp.zeros_like(pair)
    return jnp.where(low, pair, zero), jnp.where(low, zero, pair)


def attend(queries, keys, valid):
    q01, qv2 = queries
    k01, v01, kv2, ko2 = keys
    low = lanes_below(q01.shape, 64)
    q0, q1 = masked_pair(q01, low)
    q2 = jnp.where(low, qv2, jnp.zeros_like(qv2))

    def probs(q, k):
        s = jnp.where(valid, nt(q, k) * SCALE, NEG)
        e = jnp.exp(s - jnp.max(s, axis=1, keepdims=True))
        return (e / jnp.sum(e, axis=1, keepdims=True)).astype(BF)

    o0 = nn(probs(q0, k01), v01)
    o1 = nn(probs(q1, k01), v01)
    o2 = nn(probs(q2, ko2), kv2)
    return jnp.concatenate(
        [jnp.where(low, o0, o1), jnp.where(low, 0.0, o2)], axis=1
    ).astype(BF)


def attend_back(queries, keys, dob, valid):
    q01, qv2 = queries
    k01, v01, kv2, ko2 = keys
    low = lanes_below(q01.shape, 64)
    klow = lanes_below(k01.shape, 64)
    d01, d2 = dob[:, 0:128], dob[:, 128:256]
    zero = jnp.zeros_like(d2)
    d2 = jnp.where(low, zero, d2)
    q0, q1 = masked_pair(q01, low)
    d0, d1 = masked_pair(d01, low)
    q2 = jnp.where(low, qv2, jnp.zeros_like(qv2))

    def one(q, k, d, v):
        st = jnp.where(valid, nt(k, q) * SCALE, NEG)
        e = jnp.exp(st - jnp.max(st, axis=0, keepdims=True))
        p = e / jnp.sum(e, axis=0, keepdims=True)
        dp = nt(v, d)
        ds = p * (dp - jnp.sum(p * dp, axis=0, keepdims=True))
        return p.astype(BF), ds.astype(BF)

    p0, s0 = one(q0, k01, d0, v01)
    p1, s1 = one(q1, k01, d1, v01)
    p2, s2 = one(q2, ko2, d2, kv2)
    dq01 = jnp.where(low, tn(s0, k01), tn(s1, k01)) * SCALE
    dk01 = jnp.where(klow, nn(s0, q01), nn(s1, q01)) * SCALE
    dv01 = jnp.where(klow, nn(p0, d01), nn(p1, d01))
    dq2 = tn(s2, ko2) * SCALE
    dk2 = nn(s2, qv2) * SCALE
    dv2 = nn(p2, d2)
    return dq01, dk01, dv01, dq2, dk2, dv2


def pick(mine_ref, theirs_ref, into):
    n = pl.program_id(0)

    @pl.when(n < 2)
    def _():
        into[...] = mine_ref[0]

    @pl.when(n >= 2)
    def _():
        into[...] = theirs_ref[0]


def pack_kernel(wq_ref, wk_ref, wv_ref, wo_ref, wu_ref, wd_ref, attn_ref, mlp_ref):
    def turned(ref):
        size = ref.shape[0]
        at = lax.broadcasted_iota(jnp.int32, (size, size), 0)
        eye = (at == lax.broadcasted_iota(jnp.int32, (size, size), 1)).astype(BF)
        return tn(ref[...], eye).astype(BF)

    wo = turned(wo_ref)
    attn_ref[:, 0:128] = wq_ref[:, :128]
    attn_ref[:, 128:256] = wk_ref[:, :128]
    attn_ref[:, 256:384] = wv_ref[:, :128]
    attn_ref[:, 384:512] = wo[:, :128]
    attn_ref[:, 512:640] = jnp.concatenate([wq_ref[:, 128:], wv_ref[:, 128:]], axis=1)
    attn_ref[:, 640:768] = jnp.concatenate([wk_ref[:, 128:], wo[:, 128:]], axis=1)
    rows = wu_ref.shape[0]
    mlp_ref[:rows] = wu_ref[...]
    mlp_ref[rows:] = turned(wd_ref)


def spread(into, value, odd):
    zero = jnp.zeros_like(value)
    into[PATCHES:BLOCK] = zero[: BLOCK - PATCHES]
    end = HALF_AT + HALF_FIRST + HALF
    into[end:] = zero[: ROWS - end]

    @pl.when(odd == 0)
    def _():
        into[:PATCHES] = value[:PATCHES]
        into[BLOCK:end] = value[PATCHES:]

    @pl.when(odd == 1)
    def _():
        into[:PATCHES] = value[HALF : HALF + PATCHES]
        into[BLOCK : BLOCK + PATCHES] = value[HALF + PATCHES :]
        into[BLOCK + PATCHES : end] = value[:HALF]


def gather_back(into, value, odd):
    end = HALF_AT + HALF_FIRST + HALF

    @pl.when(odd == 0)
    def _():
        into[:PATCHES] = value[:PATCHES]
        into[PATCHES:] = value[BLOCK:end]

    @pl.when(odd == 1)
    def _():
        into[:HALF] = value[BLOCK + PATCHES : end]
        into[HALF : HALF + PATCHES] = value[:PATCHES]
        into[HALF + PATCHES :] = value[BLOCK : BLOCK + PATCHES]


def prep_kernel(info_ref, x_ref, c_ref, gain_ref, shift_ref, xp_ref, cp_ref, cb_ref, h_ref):
    odd = info_ref[ODD]
    spread(xp_ref, x_ref[...].astype(F32), odd)
    spread(cp_ref, c_ref[...], odd)
    cb_ref[...] = cp_ref[...].astype(BF)
    normed, _ = ln_stats(xp_ref[...])
    h_ref[...] = (normed * gain_ref[...] + shift_ref[...]).astype(BF)


def qkv_kernel(info_ref, h_ref, am_ref, at_ref, out_ref, a):
    pick(am_ref, at_ref, a)
    out_ref[0] = nn(h_ref[...], a[...]).astype(BF)


def whole_kernel(info_ref, qkv_ref, o_ref):
    valid = lanes_below((BLOCK, BLOCK), PATCHES)
    for start in FRAMES_AT:
        q01, k01, v01, qv2, ko2 = split(qkv_ref[0, start : start + BLOCK, :])
        o_ref[0, start : start + BLOCK, :] = attend((q01, qv2), (k01, v01, qv2, ko2), valid)


def half_place(shape, axis):
    at = lax.broadcasted_iota(jnp.int32, shape, axis)
    at = jnp.where(at >= HALF_ROWS, at - HALF_ROWS, at)
    return (at >= HALF_FIRST) & (at < HALF_FIRST + HALF)


def joined(mine, other):
    return tuple(jnp.concatenate([a, b], axis=0) for a, b in zip(split(mine)[1:], split(other)[1:]))


def out_kernel(
    info_ref, half_ref, other_ref, o_ref, am_ref, at_ref, x_ref, gain_ref, shift_ref, oo_ref, y_ref, h_ref, a
):
    n = pl.program_id(0)
    pick(am_ref, at_ref, a)
    q01, _, _, qv2, _ = split(half_ref[0])
    keys = joined(half_ref[0], other_ref[0])
    valid = half_place((HALF_ROWS, 2 * HALF_ROWS), 1)
    part = attend((q01, qv2), keys, valid)
    first = lax.broadcasted_iota(jnp.int32, part.shape, 0) < HALF_FIRST
    part = jnp.where(first, o_ref[0, HALF_AT:, :], part)
    oo_ref[0, :HALF_AT, :] = o_ref[0, :HALF_AT, :]
    oo_ref[0, HALF_AT:, :] = part
    o = oo_ref[0]
    z = nt(o[:, :128], a[:, 384:512]) + nt(o[:, 128:], a[:, 640:768])

    @pl.when(n == 0)
    def _():
        y_ref[...] = x_ref[...] + z

    @pl.when(n > 0)
    def _():
        y_ref[...] += z

    @pl.when(n == pl.num_programs(0) - 1)
    def _():
        normed, _ = ln_stats(y_ref[...])
        h_ref[...] = (normed * gain_ref[...] + shift_ref[...]).astype(BF)


def store_blocks(mine_ref, theirs_ref, value, me, first=0):
    n = pl.program_id(0)
    blocks = mine_ref.shape[1]
    rows = value.shape[0] // blocks
    value = value.astype(BF)

    def put(out_ref):
        for w in range(blocks):
            if blocks == 1:
                place = 0
            else:
                r = jnp.bitwise_xor(w, me)
                place = (r & 1) * (blocks // 2) + lax.shift_right_logical(r, 1)
            out_ref[0, place, first * rows : (first + 1) * rows] = value[w * rows : (w + 1) * rows]

    @pl.when(n < 2)
    def _():
        put(mine_ref)

    @pl.when(n >= 2)
    def _():
        put(theirs_ref)


def mlp_kernel(
    info_ref,
    h_ref,
    cb_ref,
    c_ref,
    y_ref,
    gain_ref,
    u_ref,
    d_ref,
    b_ref,
    act_ref,
    dmm_ref,
    dmt_ref,
    db_ref,
    dy_ref,
    dz_ref,
    sums_ref,
    ht,
    ct,
    acc,
    dub,
):
    n = pl.program_id(0)

    @pl.when(n == 0)
    def _():
        ht[...] = h_ref[...].T
        ct[...] = cb_ref[...].T

    for j in range(3):
        cols = slice(256 * j, 256 * j + 256)
        up = u_ref[:, 0, 0, :, cols].reshape(D, 256)
        down = d_ref[:, 0, 0, :, cols].reshape(D, 256)
        u = nn(h_ref[...], up) + b_ref[0, :, cols]
        big = 0.5 * (1.0 + lax.erf(u * (0.5**0.5)))
        small = jnp.exp(-0.5 * u * u) * 0.3989422804014327
        act_ref[0, :, cols] = (u * big).astype(BF)
        du = nn(cb_ref[...], down) * (big + u * small)
        db_ref[0, :, cols] = jnp.sum(du, axis=0, keepdims=True)
        dub[:, cols] = du.astype(BF)
    dh = nt(dub[...], u_ref[...].reshape(D, D))
    store_blocks(dmm_ref, dmt_ref, nn(ht[...], dub[...]), info_ref[WIDE], 0)
    store_blocks(dmm_ref, dmt_ref, nn(ct[...], act_ref[0]), info_ref[WIDE], 1)

    @pl.when(n == 0)
    def _():
        acc[...] = dh

    @pl.when(n > 0)
    def _():
        acc[...] += dh

    @pl.when(n == pl.num_programs(0) - 1)
    def _():
        normed, rstd = ln_stats(y_ref[...])
        grad = acc[...]
        c = c_ref[...]
        dy = c + ln_back(grad, normed, rstd, gain_ref[...])
        dy_ref[...] = dy
        dz_ref[...] = dy.astype(BF)
        sums_ref[0:1, :] = jnp.sum(grad * normed, axis=0, keepdims=True)
        sums_ref[1:2, :] = jnp.sum(grad, axis=0, keepdims=True)
        sums_ref[2:3, :] = jnp.sum(c, axis=0, keepdims=True)


def half_back_kernel(info_ref, dz_ref, am_ref, at_ref, half_ref, other_ref, dob_ref, own_ref, send_ref, a):
    pick(am_ref, at_ref, a)
    dz = dz_ref[...]
    dob_ref[0, :, 0:128] = nn(dz, a[:, 384:512]).astype(BF)
    dob_ref[0, :, 128:256] = nn(dz, a[:, 640:768]).astype(BF)
    dob = dob_ref[0, HALF_AT:, :]
    dob = jnp.where(half_place(dob.shape, 0), dob, jnp.zeros_like(dob))
    q01, _, _, qv2, _ = split(half_ref[0])
    keys = joined(half_ref[0], other_ref[0])
    valid = half_place((2 * HALF_ROWS, HALF_ROWS), 0)
    dq01, dk01, dv01, dq2, dk2, dv2 = attend_back((q01, qv2), keys, dob, valid)
    low = lanes_below(dq2.shape, 64)
    own_ref[0, :, 0:128] = dq01
    own_ref[0, :, 128:256] = dk01[:HALF_ROWS]
    own_ref[0, :, 256:384] = dv01[:HALF_ROWS]
    own_ref[0, :, 384:512] = jnp.zeros_like(dq01)
    own_ref[0, :, 512:640] = jnp.where(low, dq2, dv2[:HALF_ROWS])
    own_ref[0, :, 640:768] = jnp.where(low, dk2[:HALF_ROWS], 0.0)
    send_ref[0, :, 0:128] = dk01[HALF_ROWS:]
    send_ref[0, :, 128:256] = dv01[HALF_ROWS:]
    send_ref[0, :, 256:384] = jnp.where(low, 0.0, dv2[HALF_ROWS:])
    send_ref[0, :, 384:512] = jnp.where(low, dk2[HALF_ROWS:], 0.0)


def whole_back_kernel(info_ref, qkv_ref, dob_ref, out_ref):
    valid = lax.broadcasted_iota(jnp.int32, (BLOCK, BLOCK), 0) < PATCHES
    for start in FRAMES_AT:
        q01, k01, v01, qv2, ko2 = split(qkv_ref[0, start : start + BLOCK, :])
        dob = dob_ref[0, start : start + BLOCK, :]
        inside = lax.broadcasted_iota(jnp.int32, dob.shape, 0) < PATCHES
        dob = jnp.where(inside, dob, jnp.zeros_like(dob))
        dq01, dk01, dv01, dq2, dk2, dv2 = attend_back(
            (q01, qv2), (k01, v01, qv2, ko2), dob, valid
        )
        low = lanes_below(dq2.shape, 64)
        rows = slice(start, start + BLOCK)
        out_ref[0, rows, 0:128] = dq01.astype(BF)
        out_ref[0, rows, 128:256] = dk01.astype(BF)
        out_ref[0, rows, 256:384] = dv01.astype(BF)
        out_ref[0, rows, 384:512] = jnp.zeros_like(dq01).astype(BF)
        out_ref[0, rows, 512:640] = jnp.where(low, dq2, dv2).astype(BF)
        out_ref[0, rows, 640:768] = jnp.where(low, dk2, 0.0).astype(BF)


def first_kernel(
    info_ref, dqkv_ref, own_ref, recv_ref, o_ref, h_ref, dz_ref, dam_ref, dat_ref, dq_ref, ht, dt
):
    n = pl.program_id(0)

    @pl.when(n == 0)
    def _():
        ht[...] = h_ref[...].T
        dt[...] = dz_ref[...].T

    dq_ref[0, :HALF_AT] = dqkv_ref[0, :HALF_AT, :]
    own = own_ref[0]
    recv = recv_ref[0]
    whole = jnp.concatenate(
        [
            own[:, 0:128],
            own[:, 128:384] + recv[:, 0:256],
            own[:, 384:512],
            own[:, 512:768] + recv[:, 256:512],
        ],
        axis=1,
    ).astype(BF)
    first = lax.broadcasted_iota(jnp.int32, whole.shape, 0) < HALF_FIRST
    dq_ref[0, HALF_AT:] = jnp.where(first, dqkv_ref[0, HALF_AT:, :], whole)
    left = nn(ht[...], dq_ref[0, :, 0:384])
    right = nn(ht[...], dq_ref[0, :, 512:768])
    outs = nn(dt[...], o_ref[0])
    value = jnp.concatenate(
        [left, outs[:, 0:128], right[:, 0:128], right[:, 128:256] + outs[:, 128:256]], axis=1
    )
    store_blocks(dam_ref, dat_ref, value, info_ref[WIDE])


def result_kernel(info_ref, act_ref, d_ref, y_ref, bias_ref, out_ref, acc):
    n = pl.program_id(0)
    y2 = nt(act_ref[0], d_ref[...].reshape(D, D))

    @pl.when(n == 0)
    def _():
        acc[...] = y_ref[...] + y2 + bias_ref[...]

    @pl.when(n > 0)
    def _():
        acc[...] += y2

    @pl.when(n == pl.num_programs(0) - 1)
    def _():
        gather_back(out_ref, acc[...], info_ref[ODD])


def tokens_kernel(
    info_ref, dq_ref, am_ref, at_ref, x_ref, dy_ref, gain_ref, grad_ref, sums_ref, acc, weight
):
    n = pl.program_id(0)
    pick(am_ref, at_ref, weight)
    dh = nt(dq_ref[0], weight[...])

    @pl.when(n == 0)
    def _():
        acc[...] = dh

    @pl.when(n > 0)
    def _():
        acc[...] += dh

    @pl.when(n == pl.num_programs(0) - 1)
    def _():
        normed, rstd = ln_stats(x_ref[...])
        grad = acc[...]
        sums_ref[0:1, :] = jnp.sum(grad * normed, axis=0, keepdims=True)
        sums_ref[1:2, :] = jnp.sum(grad, axis=0, keepdims=True)
        gather_back(grad_ref, dy_ref[...] + ln_back(grad, normed, rstd, gain_ref[...]), info_ref[ODD])


WIDE, ORDER, ODD = 0, 1, 5


def fixed(shape):
    return pl.BlockSpec(shape, lambda n, info: (0,) * len(shape))


def panel(shape):
    return pl.BlockSpec((1,) + tuple(shape[1:]), lambda n, info: (n,) + (0,) * (len(shape) - 1))


def gathered(kind):
    def spec(shape):
        block = (shape[0], 1, 1) + tuple(shape[3:])
        return pl.BlockSpec(block, lambda n, info: (0, info[ORDER + n], kind, 0, 0))

    return spec


def mine(shape):
    return pl.BlockSpec(
        (1,) + tuple(shape[1:]), lambda n, info: (jnp.minimum(n, 1),) + (0,) * (len(shape) - 1)
    )


def theirs(shape):
    return pl.BlockSpec(
        (1,) + tuple(shape[1:]), lambda n, info: (jnp.maximum(n - 2, 0),) + (0,) * (len(shape) - 1)
    )


def crossed(shape):
    return pl.BlockSpec(
        (1,) + tuple(shape[1:]), lambda n, info: (lax.rem(n + 2, 4),) + (0,) * (len(shape) - 1)
    )


KINDS = {
    "fixed": fixed,
    "panel": panel,
    "crossed": crossed,
    "mine": mine,
    "theirs": theirs,
    "up": gathered(0),
    "down": gathered(1),
}
PANELS = 4


def call(kernel, info, ins, outs, scratch=(), flops=0, steps=PANELS):
    moved = sum(a.size * a.dtype.itemsize for a, _ in ins)
    return pl.pallas_call(
        kernel,
        grid_spec=pltpu.PrefetchScalarGridSpec(
            num_scalar_prefetch=1,
            grid=(steps,),
            in_specs=[KINDS[k](a.shape) for a, k in ins],
            out_specs=[KINDS[k](s) for s, _, k in outs],
            scratch_shapes=list(scratch),
        ),
        out_shape=[jax.ShapeDtypeStruct(s, d) for s, d, _ in outs],
        compiler_params=PARAMS,
        cost_estimate=pl.CostEstimate(
            flops=int(flops * steps), bytes_accessed=int(moved * 2), transcendentals=0
        ),
    )(info, *[a for a, _ in ins])


SMEM = pl.BlockSpec(memory_space=pltpu.SMEM)


def assemble_kernel(pieces, me_ref, *refs):
    ins, out, sem = refs[:pieces], refs[pieces], refs[pieces + 1]
    rows = ins[0].shape[1]
    copies = []
    for k in range(pieces):
        y, x, near = k // (pieces // 2), (k // 2) % 2, k % 2
        for z in range(ins[k].shape[0]):
            w = jnp.bitwise_xor(me_ref[WIDE], 2 * (2 * z + near) + x)
            at = pl.ds(pl.multiple_of(w * rows, rows), rows)
            copies.append(pltpu.make_async_copy(ins[k].at[z], out.at[y, at], sem.at[len(copies)]))
    for c in copies:
        c.start()
    for c in copies:
        c.wait()


def assemble(me, pieces):
    count = len(pieces)
    rows = pieces[0].shape[1]
    return pl.pallas_call(
        functools.partial(assemble_kernel, count),
        in_specs=[SMEM] + [pl.BlockSpec(memory_space=pl.ANY)] * count,
        out_specs=pl.BlockSpec(memory_space=pltpu.VMEM),
        out_shape=jax.ShapeDtypeStruct((2, 8 * rows, D), BF),
        scratch_shapes=[pltpu.SemaphoreType.DMA((2 * count,))],
        compiler_params=PARAMS,
        cost_estimate=pl.CostEstimate(flops=0, bytes_accessed=4 * 8 * rows * D * 2, transcendentals=0),
    )(me, *pieces)


CORE, LINE_Y, LINE_X, NEAR_Z, FAR_Z = 1, 2, 4, 8, 16


def make_swap(devices):
    def swap(value, bit):
        return lax.ppermute(value, ("wide", "narrow"), [(i, i ^ bit) for i in range(devices)])

    return swap


def after(value, *others):
    return lax.optimization_barrier((value,) + others)[0]


class Gather:
    def __init__(self, swap, me, own):
        self.swap, self.me, self.own = swap, me, own

    def lines(self):
        self.b0 = jnp.stack([self.own, self.swap(self.own, FAR_Z)])
        self.b1 = self.swap(self.b0, NEAR_Z)

    def planes(self, *wait):
        b0, b1 = self.b0, after(self.b1, *wait)
        self.x0, self.y0 = self.swap(b0, LINE_X), self.swap(b0, LINE_Y)
        self.d0 = self.swap(self.x0, LINE_Y)
        self.x1, self.y1 = self.swap(b1, LINE_X), self.swap(b1, LINE_Y)
        self.d1 = self.swap(self.y1, LINE_X)

    def finish(self, *wait):
        pieces = [self.b0, self.b1, self.x0, self.x1, self.y0, self.y1, self.d0, self.d1]
        if wait:
            pieces[0] = after(pieces[0], *wait)
        own = assemble(self.me, pieces)
        return own, self.swap(own, CORE)


def plus(left, right):
    return (left.astype(F32) + right.astype(F32)).astype(BF)


class Scatter:
    def __init__(self, swap, own, other):
        self.swap, self.own, self.state = swap, own, 0
        self.rows = own.shape[2]
        self.flight = (swap(other, CORE),)

    def step(self, *wait):
        swap = self.swap
        got = tuple(after(f, *wait) for f in self.flight) if wait else self.flight
        self.state += 1
        if self.state == 1:
            s = plus(self.own, got[0]).reshape(2, 2, 2, 2, self.rows, D)
            sa, sb = s[:, :, :, 0], s[:, :, :, 1]
            self.keep = sa[:, 0], sb[0]
            self.flight = swap(sa[:, 1], LINE_X), swap(sb[1], LINE_Y)
            return (s,)
        if self.state == 2:
            ta, tb = plus(self.keep[0], got[0]), plus(self.keep[1], got[1])
            self.keep = ta[0], tb[0]
            self.flight = swap(ta[1], LINE_Y), swap(tb[1], LINE_X)
            return (ta, tb)
        if self.state == 3:
            va, vb = plus(self.keep[0], got[0]), plus(self.keep[1], got[1])
            self.keep = va
            self.flight = (swap(vb, NEAR_Z),)
            return (va, vb)
        if self.state == 4:
            w = self.keep.astype(F32) + got[0].astype(F32)
            self.keep = w[0]
            self.flight = (swap(w[1].astype(BF), FAR_Z),)
            return (w,)
        self.result = self.keep + got[0].astype(F32)
        return (self.result,)


def body(
    tokens_in,
    cotangent,
    norm1_gain,
    norm1_shift,
    w_query,
    w_key,
    w_value,
    w_out,
    norm2_gain,
    norm2_shift,
    w_up,
    up_bias,
    w_down,
    down_bias,
    *,
    wide,
    narrow,
):
    direct = wide == 8 and narrow == 4
    wi, ni = lax.axis_index("wide"), lax.axis_index("narrow")
    twin = "crossed" if direct else "panel"
    swap = make_swap(wide * narrow)
    flipped = jnp.array([0, 2, 1, 3], jnp.int32)
    order = jnp.bitwise_xor(ni, flipped) if direct else jnp.arange(PANELS)
    me = wi if direct else jnp.zeros_like(wi)
    info = jnp.concatenate(
        [v.astype(jnp.int32) for v in (me.reshape(1), order, (ni % 2).reshape(1))]
    )
    count, rows = tokens_in.shape[0], w_up.shape[0]
    row = lambda v: v.reshape(1, D)
    room = pltpu.VMEM((D, D), BF)
    wide_row, turned = pltpu.VMEM((ROWS, D), F32), pltpu.VMEM((D, ROWS), BF)
    unit = 2 * ROWS * D * D
    act = ((PANELS, ROWS, D), BF, "panel")
    outs = ((PANELS, ROWS, 256), BF, "panel")
    tokens32, tokens16 = ((ROWS, D), F32, "fixed"), ((ROWS, D), BF, "fixed")
    result32 = ((count, D), F32, "fixed")
    sums = ((8, D), F32, "fixed")

    attn, mlp = pl.pallas_call(
        pack_kernel,
        out_shape=[jax.ShapeDtypeStruct((rows, D), BF), jax.ShapeDtypeStruct((2 * rows, D), BF)],
        compiler_params=PARAMS,
    )(w_query, w_key, w_value, w_out, w_up, w_down)
    x, c, cb, h1 = call(
        prep_kernel,
        info,
        [(tokens_in, "fixed"), (cotangent, "fixed")]
        + [(row(norm1_gain), "fixed"), (row(norm1_shift), "fixed")],
        [tokens32, tokens32, tokens16, tokens16],
        steps=1,
    )
    if direct:
        full = lax.all_gather(mlp, ("wide", "narrow"), axis=0, tiled=False)
        full = full.reshape(wide, narrow, 2, rows, D)
        ga = Gather(swap, info, attn)
        ga.lines()
        ga.planes(h1)
        a_mine, a_theirs = ga.finish()
        biases = jnp.stack([up_bias, swap(up_bias, LINE_Y)])
        biases = jnp.concatenate([biases, swap(biases, CORE)])
    else:

        def whole(v):
            return lax.all_gather(v, "narrow", axis=0, tiled=False)

        full = lax.all_gather(mlp.reshape(2, rows, D), "wide", axis=1, tiled=True)
        full = whole(full)[None]
        a_mine = whole(lax.all_gather(attn, "wide", axis=0, tiled=True))
        a_mine, a_theirs = a_mine[:2], a_mine[2:]
        biases = whole(up_bias)
    blocks = 8 if direct else 1
    grads = [((2, blocks, D // blocks, D), BF, k) for k in ("mine", "theirs")]
    grads2 = [((2, blocks, 2 * D // blocks, D), BF, k) for k in ("mine", "theirs")]
    weights_a = [(a_mine, "mine"), (a_theirs, "theirs")]

    (qkv,) = call(qkv_kernel, info, [(h1, "fixed")] + weights_a, [act], [room], flops=unit)
    half = qkv[:, HALF_AT:, :]
    other = swap(half, CORE)
    (o_part,) = call(whole_kernel, info, [(qkv, "panel")], [outs], flops=unit)
    o, y, h2 = call(
        out_kernel,
        info,
        [(half, "panel"), (other, twin), (o_part, "panel")]
        + weights_a
        + [(x, "fixed"), (row(norm2_gain), "fixed"), (row(norm2_shift), "fixed")],
        [outs, tokens32, tokens16],
        [room],
        flops=unit,
    )
    a, dm_mine, dm_theirs, grad_b, dy, dz, sums2 = call(
        mlp_kernel,
        info,
        [(h2, "fixed"), (cb, "fixed"), (c, "fixed"), (y, "fixed"), (row(norm2_gain), "fixed")]
        + [(full, "up"), (full, "down"), (biases.reshape(PANELS, 1, D), "panel")],
        [act] + grads2 + [((PANELS, 1, D), F32, "panel"), tokens32, tokens16, sums],
        [turned, turned, wide_row, pltpu.VMEM((ROWS, D), BF)],
        flops=5 * unit,
    )
    if direct:
        sm = Scatter(swap, dm_mine, dm_theirs)
    dob, own, send = call(
        half_back_kernel,
        info,
        [(dz, "fixed")] + weights_a + [(half, "panel"), (other, twin)],
        [outs, ((PANELS, HALF_ROWS, D), F32, "panel"), ((PANELS, HALF_ROWS, 512), F32, "panel")],
        [room],
        flops=unit,
    )
    recv = swap(send, CORE)
    if direct:
        dob = after(dob, *sm.step(dob))
    (dqkv,) = call(whole_back_kernel, info, [(qkv, "panel"), (dob, "panel")], [act], flops=2 * unit)
    da_mine, da_theirs, dq = call(
        first_kernel,
        info,
        [(dqkv, "panel"), (own, "panel"), (recv, twin), (o, "panel")]
        + [(h1, "fixed"), (dz, "fixed")],
        grads + [act],
        [turned, turned],
        flops=2 * unit,
    )
    if direct:
        sa = Scatter(swap, da_mine, da_theirs)
        dq = after(dq, *sm.step(dq))
    grad_x, sums1 = call(
        tokens_kernel,
        info,
        [(dq, "panel")]
        + weights_a
        + [(x, "fixed"), (dy, "fixed"), (row(norm1_gain), "fixed")],
        [result32, sums],
        [wide_row, room],
        flops=unit,
    )
    if direct:
        a = after(a, *sa.step(sums1))
    (out,) = call(
        result_kernel,
        info,
        [(a, "panel"), (full, "down"), (y, "fixed"), (row(down_bias), "fixed")],
        [result32],
        [wide_row],
        flops=unit,
    )
    grad_b = grad_b.reshape(PANELS, D)
    if direct:
        back = flipped[jnp.bitwise_xor(ni, jnp.arange(PANELS))]
        small = jnp.concatenate([sums1[:2], sums2[:3], grad_b[back]])

        def reduced(small, bit, *wait):
            small = after(small, *wait)
            return small + swap(small, bit)

        wait = sa.step(out) + sm.step(out)
        small = reduced(small, CORE, *wait)
        wait = sa.step(small) + sm.step(small)
        small = reduced(reduced(small, LINE_Y, *wait), LINE_X)
        wait = sa.step(small) + sm.step(small)
        small = reduced(reduced(small, NEAR_Z, *wait), FAR_Z)
        sa.step()
        grad_a, grad_u, grad_d = sa.result, sm.result[:rows], sm.result[rows:]
    else:

        def shard(own, other):
            v = jnp.concatenate([own, other]).reshape(PANELS, -1, D, D).astype(F32)
            v = lax.psum_scatter(v, "narrow", scatter_dimension=0, tiled=False)
            return lax.psum_scatter(v, "wide", scatter_dimension=1, tiled=True)

        (grad_a,), (grad_u, grad_d) = shard(da_mine, da_theirs), shard(dm_mine, dm_theirs)
        small = lax.psum(jnp.concatenate([sums1[:2], sums2[:3], grad_b]), ("wide", "narrow"))
    pick = lambda low, high: jnp.concatenate([grad_a[:, low : low + 128], grad_a[:, high : high + 64]], axis=1)
    return (
        out,
        grad_x,
        small[0],
        small[1],
        pick(0, 512),
        pick(128, 640),
        pick(256, 576),
        pick(384, 704).T,
        small[2],
        small[3],
        grad_u,
        lax.dynamic_index_in_dim(small, 5 + ni, 0, keepdims=False),
        grad_d.T,
        small[4],
    )


def solution(mesh):
    rows, cols, copied = P("wide", "narrow"), P("narrow", "wide"), P()
    tokens = P(("wide", "narrow"), None)
    return jax.shard_map(
        functools.partial(body, wide=mesh.shape["wide"], narrow=mesh.shape["narrow"]),
        mesh=mesh,
        in_specs=(tokens, tokens, copied, copied, rows, rows, rows, cols)
        + (copied, copied, rows, P("narrow"), cols, copied),
        out_specs=(tokens, tokens, copied, copied, rows, rows, rows, cols)
        + (copied, copied, rows, P("narrow"), cols, copied),
        check_vma=False,
    )
```

```python
import functools

import jax
import jax.numpy as jnp
from jax import lax
from jax.experimental import pallas as pl
from jax.experimental.pallas import tpu as pltpu
from jax.sharding import PartitionSpec as P

HEAD_DIM = 64
PATCHES = 196
EPS = 1e-06
D = 768
ROWS = 512
BLOCK = 208
FRAMES_AT = (0, 208)
HALF_AT = 400
HALF_ROWS = 112
HALF = PATCHES // 2
HALF_FIRST = 4
SCALE = HEAD_DIM ** (-0.5)
NEG = -1e30
VMEM = {"pack": 8, "prep": 24, "forward": 24, "mlp": 24, "back": 24, "late": 24, "merge": 16}
BF = jnp.bfloat16
F32 = jnp.float32


def nn(left, right):
    return jnp.dot(left, right, preferred_element_type=F32)


def nt(left, right):
    return lax.dot_general(left, right, (((1,), (1,)), ((), ())), preferred_element_type=F32)


def tn(left, right):
    return lax.dot_general(left, right, (((0,), (0,)), ((), ())), preferred_element_type=F32)


def lanes_below(shape, bound):
    return lax.broadcasted_iota(jnp.int32, shape, 1) < bound


def ln_stats(value):
    mean = jnp.mean(value, axis=1, keepdims=True)
    centred = value - mean
    rstd = lax.rsqrt(jnp.mean(centred * centred, axis=1, keepdims=True) + EPS)
    return centred * rstd, rstd


def ln_back(grad, normed, rstd, gain):
    scaled = grad * gain
    first = jnp.mean(scaled, axis=1, keepdims=True)
    second = jnp.mean(scaled * normed, axis=1, keepdims=True)
    return rstd * (scaled - first - normed * second)


def split(block):
    return (
        block[:, 0:128],
        block[:, 128:256],
        block[:, 256:384],
        block[:, 512:640],
        block[:, 640:768],
    )


def masked_pair(pair, low):
    zero = jnp.zeros_like(pair)
    return jnp.where(low, pair, zero), jnp.where(low, zero, pair)


def attend(queries, keys, valid):
    q01, qv2 = queries
    k01, v01, kv2, ko2 = keys
    low = lanes_below(q01.shape, 64)
    q0, q1 = masked_pair(q01, low)
    q2 = jnp.where(low, qv2, jnp.zeros_like(qv2))

    def probs(q, k):
        s = jnp.where(valid, nt(q, k) * SCALE, NEG)
        e = jnp.exp(s - jnp.max(s, axis=1, keepdims=True))
        return (e / jnp.sum(e, axis=1, keepdims=True)).astype(BF)

    o0 = nn(probs(q0, k01), v01)
    o1 = nn(probs(q1, k01), v01)
    o2 = nn(probs(q2, ko2), kv2)
    return jnp.concatenate(
        [jnp.where(low, o0, o1), jnp.where(low, 0.0, o2)], axis=1
    ).astype(BF)


def attend_back(queries, keys, dob, valid, own):
    q01, qv2 = queries
    k01, v01, kv2, ko2 = keys
    low = lanes_below(q01.shape, 64)
    d01, d2 = dob[:, 0:128], dob[:, 128:256]
    d2 = jnp.where(low, jnp.zeros_like(d2), d2)
    q0, q1 = masked_pair(q01, low)
    d0, d1 = masked_pair(d01, low)
    q2 = jnp.where(low, qv2, jnp.zeros_like(qv2))

    def one(q, k, d, v):
        st = jnp.where(valid, nt(k, q) * SCALE, NEG)
        e = jnp.exp(st - jnp.max(st, axis=0, keepdims=True))
        p = e / jnp.sum(e, axis=0, keepdims=True)
        dp = nt(v, d)
        ds = p * (dp - jnp.sum(p * dp, axis=0, keepdims=True))
        return p.astype(BF), ds.astype(BF)

    p0, s0 = one(q0, k01, d0, v01)
    p1, s1 = one(q1, k01, d1, v01)
    p2, s2 = one(q2, ko2, d2, kv2)
    low = low[:own]
    dq01 = jnp.where(low, tn(s0, k01)[:own], tn(s1, k01)[:own]) * SCALE
    dk01 = jnp.where(low, nn(s0[:own], q01), nn(s1[:own], q01)) * SCALE
    dv01 = jnp.where(low, nn(p0[:own], d01), nn(p1[:own], d01))
    dq2 = tn(s2, ko2)[:own] * SCALE
    dk2 = nn(s2[:own], qv2) * SCALE
    dv2 = nn(p2[:own], d2)
    rest = jnp.zeros_like(dq01)
    return jnp.concatenate(
        [dq01, dk01, dv01, rest, jnp.where(low, dq2, dv2), jnp.where(low, dk2, 0.0)], axis=1
    ).astype(BF)


def half_place(shape, axis):
    at = lax.broadcasted_iota(jnp.int32, shape, axis)
    at = jnp.where(at >= HALF_ROWS, at - HALF_ROWS, at)
    return (at >= HALF_FIRST) & (at < HALF_FIRST + HALF)


def pick(mine_ref, theirs_ref, into):
    n = pl.program_id(0)

    @pl.when(n < 2)
    def _():
        into[...] = mine_ref[0]

    @pl.when(n >= 2)
    def _():
        into[...] = theirs_ref[0]


def panel_copies(info_ref, sources, into, sem, start, p):
    if len(sources) == 1:
        return [pltpu.make_async_copy(sources[0].at[start + p], into.at[p], sem.at[p, 0])]
    copies = []
    for k in range(4):
        piece = sources[4 * p + k]
        rows = piece.shape[1]
        x, near = k // 2, k % 2
        for far in range(2):
            w = jnp.bitwise_xor(info_ref[WIDE], 2 * (2 * far + near) + x)
            at = pl.ds(pl.multiple_of(w * rows, rows), rows)
            copies.append(pltpu.make_async_copy(piece.at[far], into.at[p, at], sem.at[p, 2 * k + far]))
    return copies


def bring(info_ref, sources, into, sem, start, steps):
    n = pl.program_id(0)

    @pl.when(n == 0)
    def _():
        for p in range(steps):
            for c in panel_copies(info_ref, sources, into, sem, start, p):
                c.start()

    for p in range(steps):

        @pl.when(n == p)
        def _():
            for c in panel_copies(info_ref, sources, into, sem, start, p):
                c.wait()


def pack_kernel(wq_ref, wk_ref, wv_ref, wo_ref, attn_ref):
    size = wo_ref.shape[0]
    at = lax.broadcasted_iota(jnp.int32, (size, size), 0)
    eye = (at == lax.broadcasted_iota(jnp.int32, (size, size), 1)).astype(BF)
    wo = tn(wo_ref[...], eye).astype(BF)
    attn_ref[:, 0:128] = wq_ref[:, :128]
    attn_ref[:, 128:256] = wk_ref[:, :128]
    attn_ref[:, 256:384] = wv_ref[:, :128]
    attn_ref[:, 384:512] = wo[:, :128]
    attn_ref[:, 512:640] = jnp.concatenate([wq_ref[:, 128:], wv_ref[:, 128:]], axis=1)
    attn_ref[:, 640:768] = jnp.concatenate([wk_ref[:, 128:], wo[:, 128:]], axis=1)


def spread(into, value, odd):
    zero = jnp.zeros_like(value)
    into[PATCHES:BLOCK] = zero[: BLOCK - PATCHES]
    end = HALF_AT + HALF_FIRST + HALF
    into[end:] = zero[: ROWS - end]

    @pl.when(odd == 0)
    def _():
        into[:PATCHES] = value[:PATCHES]
        into[BLOCK:end] = value[PATCHES:]

    @pl.when(odd == 1)
    def _():
        into[:PATCHES] = value[HALF : HALF + PATCHES]
        into[BLOCK : BLOCK + PATCHES] = value[HALF + PATCHES :]
        into[BLOCK + PATCHES : end] = value[:HALF]


def gather_back(into, value, odd):
    end = HALF_AT + HALF_FIRST + HALF

    @pl.when(odd == 0)
    def _():
        into[:PATCHES] = value[:PATCHES]
        into[PATCHES:] = value[BLOCK:end]

    @pl.when(odd == 1)
    def _():
        into[:HALF] = value[BLOCK + PATCHES : end]
        into[HALF : HALF + PATCHES] = value[:PATCHES]
        into[HALF + PATCHES :] = value[BLOCK : BLOCK + PATCHES]


def prep_kernel(info_ref, x_ref, c_ref, xo_ref, vec_ref, xp_ref, cp_ref, cb_ref, h_ref, other):
    odd = info_ref[ODD]
    gain, shift = vec_ref[0:1, :], vec_ref[1:2, :]
    spread(xp_ref, x_ref[...].astype(F32), odd)
    spread(cp_ref, c_ref[...], odd)
    cb_ref[...] = cp_ref[...].astype(BF)
    normed, _ = ln_stats(xp_ref[...])
    h_ref[:ROWS] = (normed * gain + shift).astype(BF)
    other[...] = jnp.zeros_like(other)
    other[HALF_FIRST : HALF_FIRST + HALF] = xo_ref[...].astype(F32)
    normed, _ = ln_stats(other[...])
    h_ref[ROWS:] = (normed * gain + shift).astype(BF)


def forward_kernel(pieces, info_ref, h_ref, x_ref, vec_ref, *refs):
    sources, refs = refs[:pieces], refs[pieces:]
    qkv_ref, o_ref, a_ref, y_ref, h2_ref, w, sem = refs
    n = pl.program_id(0)
    bring(info_ref, sources, w, sem, 0, PANELS)
    a_ref[0] = w[n]
    qkv_ref[0] = nn(h_ref[...], w[n]).astype(BF)
    valid = lanes_below((BLOCK, BLOCK), PATCHES)
    for at in FRAMES_AT:
        q01, k01, v01, qv2, ko2 = split(qkv_ref[0, at : at + BLOCK, :])
        o_ref[0, at : at + BLOCK, :] = attend((q01, qv2), (k01, v01, qv2, ko2), valid)
    q01, k01, v01, qv2, ko2 = split(qkv_ref[0, HALF_AT:, :])
    valid = half_place((HALF_ROWS, 2 * HALF_ROWS), 1)
    part = attend((q01[:HALF_ROWS], qv2[:HALF_ROWS]), (k01, v01, qv2, ko2), valid)
    first = lax.broadcasted_iota(jnp.int32, (16, 256), 0) < HALF_FIRST
    o_ref[0, HALF_AT : HALF_AT + 16] = jnp.where(first, o_ref[0, HALF_AT : HALF_AT + 16], part[:16])
    o_ref[0, HALF_AT + 16 :] = part[16:]
    o = o_ref[0]
    z = nt(o[:, :128], a_ref[0, :, 384:512]) + nt(o[:, 128:], a_ref[0, :, 640:768])

    @pl.when(n == 0)
    def _():
        y_ref[...] = x_ref[...] + z

    @pl.when(n > 0)
    def _():
        y_ref[...] += z

    @pl.when(n == PANELS - 1)
    def _():
        normed, _ = ln_stats(y_ref[...])
        h2_ref[...] = (normed * vec_ref[2:3, :] + vec_ref[3:4, :]).astype(BF)


def store_blocks(out_ref, value, me, part=0):
    blocks = out_ref.shape[1]
    rows = value.shape[0] // blocks
    value = value.astype(BF)
    for w in range(blocks):
        if blocks == 1:
            place = 0
        else:
            r = jnp.bitwise_xor(w, me)
            place = (r & 2) * 2 + (r & 1) * 2 + lax.shift_right_logical(r, 2)
        out_ref[0, place, part * rows : (part + 1) * rows] = value[w * rows : (w + 1) * rows]


def mlp_kernel(last, info_ref, h_ref, cb_ref, b_ref, u_ref, d_ref, *refs):
    if last:
        base_ref, c_ref, y_ref, vec_ref, act_ref, dm_ref, db_ref, dy_ref, dz_ref, sums_ref, *refs = refs
        ht, ct, dub, acc = refs
    else:
        act_ref, dm_ref, db_ref, acc, ht, ct, dub = refs
    n = pl.program_id(0)

    @pl.when(n == 0)
    def _():
        ht[...] = h_ref[...].T
        ct[...] = cb_ref[...].T

    for j in range(3):
        cols = slice(256 * j, 256 * j + 256)
        up = u_ref[:, 0, 0, :, cols].reshape(D, 256)
        down = d_ref[:, 0, 0, :, cols].reshape(D, 256)
        u = nn(h_ref[...], up) + b_ref[0, :, cols]
        big = 0.5 * (1.0 + lax.erf(u * (0.5**0.5)))
        small = jnp.exp(-0.5 * u * u) * 0.3989422804014327
        act_ref[0, :, cols] = (u * big).astype(BF)
        du = nn(cb_ref[...], down) * (big + u * small)
        db_ref[0, :, cols] = jnp.sum(du, axis=0, keepdims=True)
        dub[:, cols] = du.astype(BF)
    dh = nt(dub[...], u_ref[...].reshape(D, D))
    store_blocks(dm_ref, nn(ht[...], dub[...]), info_ref[WIDE], 0)
    store_blocks(dm_ref, nn(ct[...], act_ref[0]), info_ref[WIDE], 1)

    @pl.when(n == 0)
    def _():
        acc[...] = base_ref[...] + dh if last else dh

    @pl.when(n == 1)
    def _():
        acc[...] += dh
        if last:
            normed, rstd = ln_stats(y_ref[...])
            grad = acc[...]
            c = c_ref[...]
            dy = c + ln_back(grad, normed, rstd, vec_ref[2:3, :])
            dy_ref[...] = dy
            dz_ref[...] = dy.astype(BF)
            sums_ref[0:1, :] = jnp.sum(grad * normed, axis=0, keepdims=True)
            sums_ref[1:2, :] = jnp.sum(grad, axis=0, keepdims=True)
            sums_ref[2:3, :] = jnp.sum(c, axis=0, keepdims=True)


def back_kernel(info_ref, dz_ref, dzo_ref, h_ref, qkv_ref, o_ref, a_ref, dam_ref, dat0_ref, dat1_ref, dq_ref, ht, dt, dob):
    n = pl.program_id(0)

    @pl.when(n == 0)
    def _():
        ht[...] = h_ref[:ROWS].T
        dt[...] = dz_ref[...].T

    for into, cols in ((0, 384), (128, 640)):
        weight = a_ref[0, :, cols : cols + 128]
        dob[:ROWS, into : into + 128] = nn(dz_ref[...], weight).astype(BF)
        dob[ROWS:, into : into + 128] = nn(dzo_ref[...], weight).astype(BF)
    valid = lax.broadcasted_iota(jnp.int32, (BLOCK, BLOCK), 0) < PATCHES
    for at in FRAMES_AT:
        q01, k01, v01, qv2, ko2 = split(qkv_ref[0, at : at + BLOCK, :])
        d = dob[at : at + BLOCK]
        inside = lax.broadcasted_iota(jnp.int32, d.shape, 0) < PATCHES
        d = jnp.where(inside, d, jnp.zeros_like(d))
        dq_ref[0, at : at + BLOCK] = attend_back(
            (q01, qv2), (k01, v01, qv2, ko2), d, valid, BLOCK
        )
    q01, k01, v01, qv2, ko2 = split(qkv_ref[0, HALF_AT:, :])
    d = dob[HALF_AT:]
    d = jnp.where(half_place(d.shape, 0), d, jnp.zeros_like(d))
    valid = half_place((2 * HALF_ROWS, 2 * HALF_ROWS), 0)
    part = attend_back((q01, qv2), (k01, v01, qv2, ko2), d, valid, HALF_ROWS)
    first = lax.broadcasted_iota(jnp.int32, (16, D), 0) < HALF_FIRST
    dq_ref[0, HALF_AT : HALF_AT + 16] = jnp.where(first, dq_ref[0, HALF_AT : HALF_AT + 16], part[:16])
    dq_ref[0, HALF_AT + 16 :] = part[16:]
    left = nn(ht[...], dq_ref[0, :, 0:384])
    right = nn(ht[...], dq_ref[0, :, 512:768])
    outs = nn(dt[...], o_ref[0])
    value = jnp.concatenate(
        [left, outs[:, 0:128], right[:, 0:128], right[:, 128:256] + outs[:, 128:256]], axis=1
    )

    @pl.when(n < 2)
    def _():
        store_blocks(dam_ref, value, info_ref[WIDE])

    @pl.when(n == 2)
    def _():
        store_blocks(dat0_ref, value, info_ref[WIDE])

    @pl.when(n == 3)
    def _():
        store_blocks(dat1_ref, value, info_ref[WIDE])


def late_kernel(
    info_ref,
    dq_ref,
    a_ref,
    actm_ref,
    actt_ref,
    d_ref,
    x_ref,
    y_ref,
    dy_ref,
    vec_ref,
    sums_ref,
    dbm_ref,
    dbt_ref,
    out_ref,
    grad_ref,
    small_ref,
    acc,
    acc2,
    left,
):
    n = pl.program_id(0)
    dh = nt(dq_ref[0], a_ref[0])

    @pl.when(n == 0)
    def _():
        acc[...] = dh

    @pl.when(n > 0)
    def _():
        acc[...] += dh

    pick(actm_ref, actt_ref, left)
    y2 = nt(left[...], d_ref[...].reshape(D, D))

    @pl.when(n == 0)
    def _():
        acc2[...] = y_ref[...] + y2 + vec_ref[4:5, :]

    @pl.when(n > 0)
    def _():
        acc2[...] += y2

    @pl.when(n == pl.num_programs(0) - 1)
    def _():
        normed, rstd = ln_stats(x_ref[...])
        grad = acc[...]
        small_ref[0:1, :] = jnp.sum(grad * normed, axis=0, keepdims=True)
        small_ref[1:2, :] = jnp.sum(grad, axis=0, keepdims=True)
        small_ref[2:5, :] = sums_ref[0:3, :]
        for j in range(PANELS):
            at = info_ref[BACK + j]

            @pl.when(at < 2)
            def _():
                small_ref[5 + j : 6 + j, :] = dbm_ref[at]

            @pl.when(at >= 2)
            def _():
                small_ref[5 + j : 6 + j, :] = dbt_ref[at - 2]

        gather_back(grad_ref, dy_ref[...] + ln_back(grad, normed, rstd, vec_ref[0:1, :]), info_ref[ODD])
        gather_back(out_ref, acc2[...], info_ref[ODD])


WIDE, ODD, BACK, ORDER = 0, 1, 2, 6
PANELS = 4


def spec(shape, kind, start):
    tail = (0,) * (len(shape) - 1)
    block = (1,) + tuple(shape[1:])
    if kind == "any":
        return pl.BlockSpec(memory_space=pl.ANY)
    if kind == "fixed":
        return pl.BlockSpec(shape, lambda n, info: (0,) + tail)
    if kind == "panel":
        return pl.BlockSpec(block, lambda n, info: (n + start,) + tail)
    if kind == "local":
        return pl.BlockSpec(block, lambda n, info: (n,) + tail)
    if kind in ("up", "down"):
        which = int(kind == "down")
        block = (shape[0], 1, 1) + tuple(shape[3:])
        return pl.BlockSpec(block, lambda n, info: (0, info[ORDER + n + start], which, 0, 0))
    if kind == "mine":
        return pl.BlockSpec(block, lambda n, info: (jnp.minimum(n, 1),) + tail)
    return pl.BlockSpec(block, lambda n, info: (jnp.maximum(n - 2, 0),) + tail)


def call(kernel, info, ins, outs, scratch=(), units=0, steps=PANELS, start=0, vmem="back"):
    moved = sum(a.size * a.dtype.itemsize for a, _ in ins)
    return pl.pallas_call(
        kernel,
        grid_spec=pltpu.PrefetchScalarGridSpec(
            num_scalar_prefetch=1,
            grid=(steps,),
            in_specs=[spec(a.shape, k, start) for a, k in ins],
            out_specs=[spec(s, k, start) for s, _, k in outs],
            scratch_shapes=list(scratch),
        ),
        out_shape=[jax.ShapeDtypeStruct(s, d) for s, d, _ in outs],
        compiler_params=pltpu.CompilerParams(vmem_limit_bytes=VMEM[vmem] << 20),
        cost_estimate=pl.CostEstimate(
            flops=int(2 * ROWS * D * D * units * steps), bytes_accessed=int(moved * 2), transcendentals=0
        ),
    )(info, *[a for a, _ in ins])


CORE, LINE_Y, LINE_X, NEAR_Z, FAR_Z = 1, 2, 4, 8, 16


def make_swap(devices):
    def swap(value, bit):
        return lax.ppermute(value, ("wide", "narrow"), [(i, i ^ bit) for i in range(devices)])

    return swap


def after(value, *others):
    return lax.optimization_barrier((value,) + others)[0] if others else value


class Gather:
    def __init__(self, swap, own):
        self.swap, self.own = swap, own

    def far(self, *wait):
        own = after(self.own, *wait)
        self.b0 = jnp.stack([own, self.swap(own, FAR_Z)])

    def near(self, *wait):
        self.b1 = self.swap(after(self.b0, *wait), NEAR_Z)

    def planes0(self, *wait):
        b0 = after(self.b0, *wait)
        self.x0, self.y0 = self.swap(b0, LINE_X), self.swap(b0, LINE_Y)

    def planes1(self, *wait):
        b1 = after(self.b1, *wait)
        self.x1, self.y1 = self.swap(b1, LINE_X), self.swap(b1, LINE_Y)

    def corners(self, *wait):
        x0, y1 = after(self.x0, *wait), after(self.y1, *wait)
        self.d0, self.d1 = self.swap(x0, LINE_Y), self.swap(y1, LINE_X)

    def mine(self):
        return [self.b0, self.b1, self.x0, self.x1, self.y0, self.y1, self.d0, self.d1]

    def theirs(self):
        return [self.swap(v, CORE) for v in self.mine()]


def merge_kernel(own_ref, *refs):
    got_refs, (keep_a, send_a, keep_b, send_b) = refs[:-4], refs[-4:]
    y, k = pl.program_id(0), pl.program_id(1)
    got = got_refs[0][...]
    if len(got_refs) == 2:
        got = jnp.where(y == 0, got, got_refs[1][...])
    value = (own_ref[...].astype(F32) + got.astype(F32)).astype(BF)

    @pl.when(k == 0)
    def _():
        keep_a[...] = value

    @pl.when(k == 1)
    def _():
        send_a[...] = value

    @pl.when((k >= 2) & (y == 0))
    def _():
        keep_b[...] = value

    @pl.when((k >= 2) & (y == 1))
    def _():
        send_b[...] = value


def merge(own, *got):
    rows = own.shape[2]
    block = (1, 2, rows, D)
    taken = pl.BlockSpec(block, lambda y, k: (y, k, 0, 0))
    by_y = pl.BlockSpec(block, lambda y, k: (y, 0, 0, 0))
    first = pl.BlockSpec(block, lambda y, k: (jnp.where(y == 0, jnp.maximum(k - 2, 0), 1), 0, 0, 0))
    second = pl.BlockSpec(block, lambda y, k: (jnp.where(y == 0, 0, jnp.maximum(k - 2, 0)), 0, 0, 0))
    size = own.size * 2
    gots = [taken]
    if len(got) == 2:
        gots = [
            pl.BlockSpec(block, lambda y, k: (0, jnp.where(y == 0, k, 3), 0, 0)),
            pl.BlockSpec(block, lambda y, k: (0, jnp.where(y == 0, 0, k), 0, 0)),
        ]
    return pl.pallas_call(
        merge_kernel,
        grid=(2, 4),
        in_specs=[taken] + gots,
        out_specs=[by_y, by_y, first, second],
        out_shape=[jax.ShapeDtypeStruct((2, 2, rows, D), BF)] * 4,
        compiler_params=pltpu.CompilerParams(vmem_limit_bytes=VMEM["merge"] << 20),
        cost_estimate=pl.CostEstimate(flops=0, bytes_accessed=3 * size, transcendentals=0),
    )(own, *got)


def total(*parts):
    value = parts[0].astype(F32)
    for p in parts[1:]:
        value = value + p.astype(F32)
    return value


class Scatter:
    def __init__(self, swap, *other):
        self.swap, self.state = swap, 0
        self.flight = tuple(swap(v, CORE) for v in other)

    def step(self, *wait, own=None):
        swap = self.swap
        got = tuple(after(f, *wait) for f in self.flight)
        self.state += 1
        if self.state == 1:
            self.a, send_a, self.b, send_b = merge(own, *got)
            self.flight = swap(send_a, LINE_X), swap(send_b, LINE_Y)
            return (send_a, send_b)
        if self.state == 2:
            send_a = total(self.a[1], got[0][1]).astype(BF)
            send_b = total(self.b[1], got[1][1]).astype(BF)
            self.a, self.b = (self.a[0], got[0][0]), (self.b[0], got[1][0])
            self.flight = swap(send_a, LINE_Y), swap(send_b, LINE_X)
            return (send_a, send_b)
        if self.state == 3:
            self.a = self.a + (got[0],)
            send = total(*self.b, got[1]).astype(BF)
            self.flight = (swap(send, NEAR_Z),)
            return (send,)
        if self.state == 4:
            self.a = self.a + (got[0],)
            send = total(*(p[1] for p in self.a)).astype(BF)
            self.flight = (swap(send, FAR_Z),)
            return (send,)
        self.result = total(*(p[0] for p in self.a), got[0])
        return (self.result,)


def body(
    tokens_in,
    cotangent,
    norm1_gain,
    norm1_shift,
    w_query,
    w_key,
    w_value,
    w_out,
    norm2_gain,
    norm2_shift,
    w_up,
    up_bias,
    w_down,
    down_bias,
    *,
    wide,
    narrow,
):
    direct = wide == 8 and narrow == 4
    wi, ni = lax.axis_index("wide"), lax.axis_index("narrow")
    swap = make_swap(wide * narrow)
    flipped = jnp.array([0, 2, 1, 3], jnp.int32)
    places = jnp.arange(PANELS, dtype=jnp.int32)
    back = flipped[jnp.bitwise_xor(ni, places)] if direct else places
    order = jnp.bitwise_xor(ni, flipped) if direct else places
    me = wi if direct else jnp.zeros_like(wi)
    info = jnp.concatenate(
        [v.astype(jnp.int32) for v in (me.reshape(1), (ni % 2).reshape(1), back, order)]
    )
    count, rows = tokens_in.shape[0], w_up.shape[0]
    vecs = jnp.stack([norm1_gain, norm1_shift, norm2_gain, norm2_shift, down_bias] + [down_bias] * 3)
    wide_row, turned = pltpu.VMEM((ROWS, D), F32), pltpu.VMEM((D, ROWS), BF)
    tokens32, tokens16 = ((ROWS, D), F32, "fixed"), ((ROWS, D), BF, "fixed")
    result32 = ((count, D), F32, "fixed")
    sums = ((8, D), F32, "fixed")
    blocks = 8 if direct else 1
    grads_a, grads_m = (2, blocks, D // blocks, D), (2, blocks, 2 * D // blocks, D)

    mlp = jnp.concatenate([w_up, w_down.T])
    if direct:
        full = lax.all_gather(mlp, ("wide", "narrow"), axis=0, tiled=False)
        full = full.reshape(wide, narrow, 2, rows, D)
    (attn,) = pl.pallas_call(
        pack_kernel,
        out_shape=[jax.ShapeDtypeStruct((rows, D), BF)],
        compiler_params=pltpu.CompilerParams(vmem_limit_bytes=VMEM["pack"] << 20),
    )(w_query, w_key, w_value, w_out)
    shared = jnp.where(ni % 2 == 1, tokens_in[:HALF], tokens_in[count - HALF :])
    shared = swap(shared, CORE)
    x, c, cb, h1 = call(
        prep_kernel,
        info,
        [(tokens_in, "fixed"), (cotangent, "fixed"), (shared, "fixed"), (vecs, "fixed")],
        [tokens32, tokens32, tokens16, ((ROWS + HALF_ROWS, D), BF, "fixed")],
        [pltpu.VMEM((HALF_ROWS, D), F32)],
        steps=1,
        vmem="prep",
    )
    if direct:
        ga = Gather(swap, attn)
        ga.far()
        ga.near()
        ga.planes0()
        ga.planes1(h1)
        ga.corners()
        sources = ga.mine() + ga.theirs()
        b_y, b_c = swap(after(up_bias, ga.d0, ga.d1), LINE_Y), swap(up_bias, CORE)
    else:

        def whole(v):
            return lax.all_gather(v, "narrow", axis=0, tiled=False)

        sources = [whole(lax.all_gather(attn, "wide", axis=0, tiled=True))]
        full = lax.all_gather(mlp.reshape(2, rows, D), "wide", axis=1, tiled=True)
        full = whole(full)[None]
        biases = whole(up_bias)
    qkv, o, a, y, h2 = call(
        functools.partial(forward_kernel, len(sources)),
        info,
        [(h1, "fixed"), (x, "fixed"), (vecs, "fixed")] + [(v, "any") for v in sources],
        [((PANELS, ROWS + HALF_ROWS, D), BF, "panel"), ((PANELS, ROWS, 256), BF, "panel")]
        + [((PANELS, D, D), BF, "panel"), tokens32, tokens16],
        [pltpu.VMEM((PANELS, D, D), BF), pltpu.SemaphoreType.DMA((PANELS, 8))],
        units=2,
        vmem="forward",
    )

    if direct:
        b_y = after(b_y, h2)
        biases = jnp.stack([up_bias, b_y, b_c, swap(b_y, CORE)])
    biases = biases.reshape(PANELS, 1, D)

    def mlp_part(start, more_in, more_out, more_scratch):
        return call(
            functools.partial(mlp_kernel, not start),
            info,
            [(h2, "fixed"), (cb, "fixed"), (biases, "panel"), (full, "up"), (full, "down")] + more_in,
            [((2, ROWS, D), BF, "local"), (grads_m, BF, "local"), ((2, 1, D), F32, "local")] + more_out,
            [turned, turned, pltpu.VMEM((ROWS, D), BF)] + more_scratch,
            units=5,
            steps=2,
            start=start,
            vmem="mlp",
        )

    act_t, dm_t, db_t, acc = mlp_part(2, [], [tokens32], [])
    if direct:
        sm = Scatter(swap, dm_t)
    act_m, dm_m, db_m, dy, dz, sums2 = mlp_part(
        0,
        [(acc, "fixed"), (c, "fixed"), (y, "fixed"), (vecs, "fixed")],
        [tokens32, tokens16, sums],
        [wide_row],
    )
    dzo = swap(dz[HALF_AT:], CORE)
    if direct:
        dz = after(dz, *sm.step(dz, own=dm_m))

    grads_one = ((1,) + grads_a[1:], BF, "fixed")
    da_m, *da_t, dq = call(
        back_kernel,
        info,
        [(dz, "fixed"), (dzo, "fixed"), (h1, "fixed"), (qkv, "panel"), (o, "panel"), (a, "panel")],
        [(grads_a, BF, "mine"), grads_one, grads_one, ((PANELS, ROWS, D), BF, "panel")],
        [turned, turned, pltpu.VMEM((ROWS + HALF_ROWS, 256), BF)],
        units=4,
    )
    if direct:
        sa = Scatter(swap, *da_t)
        sent = sm.step(dq)
        dq = after(dq, *sent, *sa.step(*sent, own=da_m))
    out, grad_x, small = call(
        late_kernel,
        info,
        [(dq, "panel"), (a, "panel"), (act_m, "mine"), (act_t, "theirs")]
        + [(full, "down"), (x, "fixed"), (y, "fixed"), (dy, "fixed")]
        + [(vecs, "fixed"), (sums2, "fixed"), (db_m, "fixed"), (db_t, "fixed")],
        [result32, result32, ((16, D), F32, "fixed")],
        [wide_row, wide_row, pltpu.VMEM((ROWS, D), BF)],
        units=2,
        vmem="late",
    )
    if direct:

        def reduced(small, bit, *wait):
            small = after(small, *wait)
            return small + swap(small, bit)

        wait = sa.step(small)
        small = reduced(reduced(small, CORE, *wait), FAR_Z)
        wait = sm.step(small)
        small = reduced(small, LINE_X, *sa.step(small, *wait))
        wait = sm.step(small)
        small = reduced(reduced(small, LINE_Y, *sa.step(small, *wait)), NEAR_Z)
        sm.step(), sa.step()
        grad_a, grad_u, grad_d = sa.result, sm.result[:rows], sm.result[rows:]
    else:

        def shard(own, other):
            v = jnp.concatenate([own, other]).reshape(PANELS, -1, D, D).astype(F32)
            v = lax.psum_scatter(v, "narrow", scatter_dimension=0, tiled=False)
            return lax.psum_scatter(v, "wide", scatter_dimension=1, tiled=True)

        (grad_a,), (grad_u, grad_d) = shard(da_m, jnp.concatenate(da_t)), shard(dm_m, dm_t)
        small = lax.psum(small, ("wide", "narrow"))
    pick_lanes = lambda low, high: jnp.concatenate(
        [grad_a[:, low : low + 128], grad_a[:, high : high + 64]], axis=1
    )
    return (
        out,
        grad_x,
        small[0],
        small[1],
        pick_lanes(0, 512),
        pick_lanes(128, 640),
        pick_lanes(256, 576),
        pick_lanes(384, 704).T,
        small[2],
        small[3],
        grad_u,
        lax.dynamic_index_in_dim(small, 5 + ni, 0, keepdims=False),
        grad_d.T,
        small[4],
    )


def solution(mesh):
    rows, cols, copied = P("wide", "narrow"), P("narrow", "wide"), P()
    tokens = P(("wide", "narrow"), None)
    return jax.shard_map(
        functools.partial(body, wide=mesh.shape["wide"], narrow=mesh.shape["narrow"]),
        mesh=mesh,
        in_specs=(tokens, tokens, copied, copied, rows, rows, rows, cols)
        + (copied, copied, rows, P("narrow"), cols, copied),
        out_specs=(tokens, tokens, copied, copied, rows, rows, rows, cols)
        + (copied, copied, rows, P("narrow"), cols, copied),
        check_vma=False,
    )
```

```python
import functools

import jax
import jax.numpy as jnp
from jax import lax
from jax.experimental import pallas as pl
from jax.experimental.pallas import tpu as pltpu
from jax.sharding import PartitionSpec as P

HEAD_DIM = 64
PATCHES = 196
EPS = 1e-06
D = 768
ROWS = 512
BLOCK = 208
FRAMES_AT = (0, 208)
HALF_AT = 400
HALF_ROWS = 112
HALF = PATCHES // 2
HALF_FIRST = 4
SCALE = HEAD_DIM ** (-0.5)
NEG = -1e30
VMEM = {"pack": 4, "prep": 8, "forward": 16, "mlp": 16, "back": 16, "late": 16, "merge": 8}
BF = jnp.bfloat16
F32 = jnp.float32


def nn(left, right):
    return jnp.dot(left, right, preferred_element_type=F32)


def nt(left, right):
    return lax.dot_general(left, right, (((1,), (1,)), ((), ())), preferred_element_type=F32)


def tn(left, right):
    return lax.dot_general(left, right, (((0,), (0,)), ((), ())), preferred_element_type=F32)


def lanes_below(shape, bound):
    return lax.broadcasted_iota(jnp.int32, shape, 1) < bound


def ln_stats(value):
    mean = jnp.mean(value, axis=1, keepdims=True)
    centred = value - mean
    rstd = lax.rsqrt(jnp.mean(centred * centred, axis=1, keepdims=True) + EPS)
    return centred * rstd, rstd


def ln_back(grad, normed, rstd, gain):
    scaled = grad * gain
    first = jnp.mean(scaled, axis=1, keepdims=True)
    second = jnp.mean(scaled * normed, axis=1, keepdims=True)
    return rstd * (scaled - first - normed * second)


def split(block):
    return (
        block[:, 0:128],
        block[:, 128:256],
        block[:, 256:384],
        block[:, 512:640],
        block[:, 640:768],
    )


def masked_pair(pair, low):
    zero = jnp.zeros_like(pair)
    return jnp.where(low, pair, zero), jnp.where(low, zero, pair)


def attend(queries, keys, valid):
    q01, qv2 = queries
    k01, v01, kv2, ko2 = keys
    low = lanes_below(q01.shape, 64)
    q0, q1 = masked_pair(q01, low)
    q2 = jnp.where(low, qv2, jnp.zeros_like(qv2))

    def probs(q, k):
        s = jnp.where(valid, nt(q, k) * SCALE, NEG)
        e = jnp.exp(s - jnp.max(s, axis=1, keepdims=True))
        return (e / jnp.sum(e, axis=1, keepdims=True)).astype(BF)

    o0 = nn(probs(q0, k01), v01)
    o1 = nn(probs(q1, k01), v01)
    o2 = nn(probs(q2, ko2), kv2)
    return jnp.concatenate(
        [jnp.where(low, o0, o1), jnp.where(low, 0.0, o2)], axis=1
    ).astype(BF)


def attend_back(queries, keys, dob, valid, own):
    q01, qv2 = queries
    k01, v01, kv2, ko2 = keys
    low = lanes_below(q01.shape, 64)
    d01, d2 = dob[:, 0:128], dob[:, 128:256]
    d2 = jnp.where(low, jnp.zeros_like(d2), d2)
    q0, q1 = masked_pair(q01, low)
    d0, d1 = masked_pair(d01, low)
    q2 = jnp.where(low, qv2, jnp.zeros_like(qv2))

    def one(q, k, d, v):
        st = jnp.where(valid, nt(k, q) * SCALE, NEG)
        e = jnp.exp(st - jnp.max(st, axis=0, keepdims=True))
        p = e / jnp.sum(e, axis=0, keepdims=True)
        dp = nt(v, d)
        ds = p * (dp - jnp.sum(p * dp, axis=0, keepdims=True))
        return p.astype(BF), ds.astype(BF)

    p0, s0 = one(q0, k01, d0, v01)
    p1, s1 = one(q1, k01, d1, v01)
    p2, s2 = one(q2, ko2, d2, kv2)
    low = low[:own]
    dq01 = jnp.where(low, tn(s0, k01)[:own], tn(s1, k01)[:own]) * SCALE
    dk01 = jnp.where(low, nn(s0[:own], q01), nn(s1[:own], q01)) * SCALE
    dv01 = jnp.where(low, nn(p0[:own], d01), nn(p1[:own], d01))
    dq2 = tn(s2, ko2)[:own] * SCALE
    dk2 = nn(s2[:own], qv2) * SCALE
    dv2 = nn(p2[:own], d2)
    rest = jnp.zeros_like(dq01)
    return jnp.concatenate(
        [dq01, dk01, dv01, rest, jnp.where(low, dq2, dv2), jnp.where(low, dk2, 0.0)], axis=1
    ).astype(BF)


def half_place(shape, axis):
    at = lax.broadcasted_iota(jnp.int32, shape, axis)
    at = jnp.where(at >= HALF_ROWS, at - HALF_ROWS, at)
    return (at >= HALF_FIRST) & (at < HALF_FIRST + HALF)


def pick(mine_ref, theirs_ref, into):
    n = pl.program_id(0)

    @pl.when(n < 2)
    def _():
        into[...] = mine_ref[0]

    @pl.when(n >= 2)
    def _():
        into[...] = theirs_ref[0]


def panel_copies(info_ref, sources, into, sem, start, p):
    if len(sources) == 1:
        return [pltpu.make_async_copy(sources[0].at[start + p], into.at[p], sem.at[p, 0])]
    copies = []
    for k in range(4):
        piece = sources[4 * p + k]
        rows = piece.shape[1]
        x, near = k // 2, k % 2
        for far in range(2):
            w = jnp.bitwise_xor(info_ref[WIDE], 2 * (2 * far + near) + x)
            at = pl.ds(pl.multiple_of(w * rows, rows), rows)
            copies.append(pltpu.make_async_copy(piece.at[far], into.at[p, at], sem.at[p, 2 * k + far]))
    return copies


def bring(info_ref, sources, into, sem, start, steps):
    n = pl.program_id(0)

    @pl.when(n == 0)
    def _():
        for p in range(steps):
            for c in panel_copies(info_ref, sources, into, sem, start, p):
                c.start()

    for p in range(steps):

        @pl.when(n == p)
        def _():
            for c in panel_copies(info_ref, sources, into, sem, start, p):
                c.wait()


def pack_kernel(wq_ref, wk_ref, wv_ref, wo_ref, attn_ref):
    size = wo_ref.shape[0]
    at = lax.broadcasted_iota(jnp.int32, (size, size), 0)
    eye = (at == lax.broadcasted_iota(jnp.int32, (size, size), 1)).astype(BF)
    wo = tn(wo_ref[...], eye).astype(BF)
    attn_ref[:, 0:128] = wq_ref[:, :128]
    attn_ref[:, 128:256] = wk_ref[:, :128]
    attn_ref[:, 256:384] = wv_ref[:, :128]
    attn_ref[:, 384:512] = wo[:, :128]
    attn_ref[:, 512:640] = jnp.concatenate([wq_ref[:, 128:], wv_ref[:, 128:]], axis=1)
    attn_ref[:, 640:768] = jnp.concatenate([wk_ref[:, 128:], wo[:, 128:]], axis=1)


def spread(into, value, odd):
    zero = jnp.zeros_like(value)
    into[PATCHES:BLOCK] = zero[: BLOCK - PATCHES]
    end = HALF_AT + HALF_FIRST + HALF
    into[end:] = zero[: ROWS - end]

    @pl.when(odd == 0)
    def _():
        into[:PATCHES] = value[:PATCHES]
        into[BLOCK:end] = value[PATCHES:]

    @pl.when(odd == 1)
    def _():
        into[:PATCHES] = value[HALF : HALF + PATCHES]
        into[BLOCK : BLOCK + PATCHES] = value[HALF + PATCHES :]
        into[BLOCK + PATCHES : end] = value[:HALF]


def gather_back(into, value, odd):
    end = HALF_AT + HALF_FIRST + HALF

    @pl.when(odd == 0)
    def _():
        into[:PATCHES] = value[:PATCHES]
        into[PATCHES:] = value[BLOCK:end]

    @pl.when(odd == 1)
    def _():
        into[:HALF] = value[BLOCK + PATCHES : end]
        into[HALF : HALF + PATCHES] = value[:PATCHES]
        into[HALF + PATCHES :] = value[BLOCK : BLOCK + PATCHES]


def prep_kernel(info_ref, x_ref, c_ref, xo_ref, vec_ref, xp_ref, cp_ref, cb_ref, h_ref, other):
    odd = info_ref[ODD]
    gain, shift = vec_ref[0:1, :], vec_ref[1:2, :]
    spread(xp_ref, x_ref[...].astype(F32), odd)
    spread(cp_ref, c_ref[...], odd)
    cb_ref[...] = cp_ref[...].astype(BF)
    normed, _ = ln_stats(xp_ref[...])
    h_ref[:ROWS] = (normed * gain + shift).astype(BF)
    other[...] = jnp.zeros_like(other)
    other[HALF_FIRST : HALF_FIRST + HALF] = xo_ref[...].astype(F32)
    normed, _ = ln_stats(other[...])
    h_ref[ROWS:] = (normed * gain + shift).astype(BF)


def forward_kernel(pieces, info_ref, h_ref, x_ref, vec_ref, *refs):
    sources, refs = refs[:pieces], refs[pieces:]
    qkv_ref, o_ref, a_ref, y_ref, h2_ref, w, sem = refs
    n = pl.program_id(0)
    bring(info_ref, sources, w, sem, 0, PANELS)
    a_ref[0] = w[n]
    qkv_ref[0] = nn(h_ref[...], w[n]).astype(BF)
    valid = lanes_below((BLOCK, BLOCK), PATCHES)
    for at in FRAMES_AT:
        q01, k01, v01, qv2, ko2 = split(qkv_ref[0, at : at + BLOCK, :])
        o_ref[0, at : at + BLOCK, :] = attend((q01, qv2), (k01, v01, qv2, ko2), valid)
    q01, k01, v01, qv2, ko2 = split(qkv_ref[0, HALF_AT:, :])
    valid = half_place((HALF_ROWS, 2 * HALF_ROWS), 1)
    part = attend((q01[:HALF_ROWS], qv2[:HALF_ROWS]), (k01, v01, qv2, ko2), valid)
    first = lax.broadcasted_iota(jnp.int32, (16, 256), 0) < HALF_FIRST
    o_ref[0, HALF_AT : HALF_AT + 16] = jnp.where(first, o_ref[0, HALF_AT : HALF_AT + 16], part[:16])
    o_ref[0, HALF_AT + 16 :] = part[16:]
    o = o_ref[0]
    z = nt(o[:, :128], a_ref[0, :, 384:512]) + nt(o[:, 128:], a_ref[0, :, 640:768])

    @pl.when(n == 0)
    def _():
        y_ref[...] = x_ref[...] + z

    @pl.when(n > 0)
    def _():
        y_ref[...] += z

    @pl.when(n == PANELS - 1)
    def _():
        normed, _ = ln_stats(y_ref[...])
        h2_ref[...] = (normed * vec_ref[2:3, :] + vec_ref[3:4, :]).astype(BF)


def store_blocks(out_ref, value, me, part=0):
    blocks = out_ref.shape[1]
    rows = value.shape[0] // blocks
    value = value.astype(BF)
    for w in range(blocks):
        if blocks == 1:
            place = 0
        else:
            r = jnp.bitwise_xor(w, me)
            place = (r & 2) * 2 + (r & 1) * 2 + lax.shift_right_logical(r, 2)
        out_ref[0, place, part * rows : (part + 1) * rows] = value[w * rows : (w + 1) * rows]


def mlp_kernel(last, info_ref, h_ref, cb_ref, b_ref, u_ref, d_ref, *refs):
    if last:
        base_ref, c_ref, y_ref, vec_ref, act_ref, dm_ref, db_ref, dy_ref, dz_ref, sums_ref, *refs = refs
        ht, ct, dub, acc = refs
    else:
        act_ref, dm_ref, db_ref, acc, ht, ct, dub = refs
    n = pl.program_id(0)

    @pl.when(n == 0)
    def _():
        ht[...] = h_ref[...].T
        ct[...] = cb_ref[...].T

    for j in range(3):
        cols = slice(256 * j, 256 * j + 256)
        up = u_ref[:, 0, 0, :, cols].reshape(D, 256)
        down = d_ref[:, 0, 0, :, cols].reshape(D, 256)
        u = nn(h_ref[...], up) + b_ref[0, :, cols]
        big = 0.5 * (1.0 + lax.erf(u * (0.5**0.5)))
        small = jnp.exp(-0.5 * u * u) * 0.3989422804014327
        act_ref[0, :, cols] = (u * big).astype(BF)
        du = nn(cb_ref[...], down) * (big + u * small)
        db_ref[0, :, cols] = jnp.sum(du, axis=0, keepdims=True)
        dub[:, cols] = du.astype(BF)
    dh = nt(dub[...], u_ref[...].reshape(D, D))
    store_blocks(dm_ref, nn(ht[...], dub[...]), info_ref[WIDE], 0)
    store_blocks(dm_ref, nn(ct[...], act_ref[0]), info_ref[WIDE], 1)

    @pl.when(n == 0)
    def _():
        acc[...] = base_ref[...] + dh if last else dh

    @pl.when(n == 1)
    def _():
        acc[...] += dh
        if last:
            normed, rstd = ln_stats(y_ref[...])
            grad = acc[...]
            c = c_ref[...]
            dy = c + ln_back(grad, normed, rstd, vec_ref[2:3, :])
            dy_ref[...] = dy
            dz_ref[...] = dy.astype(BF)
            sums_ref[0:1, :] = jnp.sum(grad * normed, axis=0, keepdims=True)
            sums_ref[1:2, :] = jnp.sum(grad, axis=0, keepdims=True)
            sums_ref[2:3, :] = jnp.sum(c, axis=0, keepdims=True)


def back_kernel(info_ref, dz_ref, dzo_ref, h_ref, qkv_ref, o_ref, a_ref, dam_ref, dat0_ref, dat1_ref, dq_ref, ht, dt, dob):
    n = pl.program_id(0)

    @pl.when(n == 0)
    def _():
        ht[...] = h_ref[:ROWS].T
        dt[...] = dz_ref[...].T

    for into, cols in ((0, 384), (128, 640)):
        weight = a_ref[0, :, cols : cols + 128]
        dob[:ROWS, into : into + 128] = nn(dz_ref[...], weight).astype(BF)
        dob[ROWS:, into : into + 128] = nn(dzo_ref[...], weight).astype(BF)
    valid = lax.broadcasted_iota(jnp.int32, (BLOCK, BLOCK), 0) < PATCHES
    for at in FRAMES_AT:
        q01, k01, v01, qv2, ko2 = split(qkv_ref[0, at : at + BLOCK, :])
        d = dob[at : at + BLOCK]
        inside = lax.broadcasted_iota(jnp.int32, d.shape, 0) < PATCHES
        d = jnp.where(inside, d, jnp.zeros_like(d))
        dq_ref[0, at : at + BLOCK] = attend_back(
            (q01, qv2), (k01, v01, qv2, ko2), d, valid, BLOCK
        )
    q01, k01, v01, qv2, ko2 = split(qkv_ref[0, HALF_AT:, :])
    d = dob[HALF_AT:]
    d = jnp.where(half_place(d.shape, 0), d, jnp.zeros_like(d))
    valid = half_place((2 * HALF_ROWS, 2 * HALF_ROWS), 0)
    part = attend_back((q01, qv2), (k01, v01, qv2, ko2), d, valid, HALF_ROWS)
    first = lax.broadcasted_iota(jnp.int32, (16, D), 0) < HALF_FIRST
    dq_ref[0, HALF_AT : HALF_AT + 16] = jnp.where(first, dq_ref[0, HALF_AT : HALF_AT + 16], part[:16])
    dq_ref[0, HALF_AT + 16 :] = part[16:]
    left = nn(ht[...], dq_ref[0, :, 0:384])
    right = nn(ht[...], dq_ref[0, :, 512:768])
    outs = nn(dt[...], o_ref[0])
    value = jnp.concatenate(
        [left, outs[:, 0:128], right[:, 0:128], right[:, 128:256] + outs[:, 128:256]], axis=1
    )

    @pl.when(n < 2)
    def _():
        store_blocks(dam_ref, value, info_ref[WIDE])

    @pl.when(n == 2)
    def _():
        store_blocks(dat0_ref, value, info_ref[WIDE])

    @pl.when(n == 3)
    def _():
        store_blocks(dat1_ref, value, info_ref[WIDE])


def late_kernel(
    info_ref,
    dq_ref,
    a_ref,
    actm_ref,
    actt_ref,
    d_ref,
    x_ref,
    y_ref,
    dy_ref,
    vec_ref,
    sums_ref,
    dbm_ref,
    dbt_ref,
    out_ref,
    grad_ref,
    small_ref,
    acc,
    acc2,
    left,
):
    n = pl.program_id(0)
    dh = nt(dq_ref[0], a_ref[0])

    @pl.when(n == 0)
    def _():
        acc[...] = dh

    @pl.when(n > 0)
    def _():
        acc[...] += dh

    pick(actm_ref, actt_ref, left)
    y2 = nt(left[...], d_ref[...].reshape(D, D))

    @pl.when(n == 0)
    def _():
        acc2[...] = y_ref[...] + y2 + vec_ref[4:5, :]

    @pl.when(n > 0)
    def _():
        acc2[...] += y2

    @pl.when(n == pl.num_programs(0) - 1)
    def _():
        normed, rstd = ln_stats(x_ref[...])
        grad = acc[...]
        small_ref[0:1, :] = jnp.sum(grad * normed, axis=0, keepdims=True)
        small_ref[1:2, :] = jnp.sum(grad, axis=0, keepdims=True)
        small_ref[2:5, :] = sums_ref[0:3, :]
        for j in range(PANELS):
            at = info_ref[BACK + j]

            @pl.when(at < 2)
            def _():
                small_ref[5 + j : 6 + j, :] = dbm_ref[at]

            @pl.when(at >= 2)
            def _():
                small_ref[5 + j : 6 + j, :] = dbt_ref[at - 2]

        gather_back(grad_ref, dy_ref[...] + ln_back(grad, normed, rstd, vec_ref[0:1, :]), info_ref[ODD])
        gather_back(out_ref, acc2[...], info_ref[ODD])


WIDE, ODD, BACK, ORDER = 0, 1, 2, 6
PANELS = 4


def spec(shape, kind, start):
    tail = (0,) * (len(shape) - 1)
    block = (1,) + tuple(shape[1:])
    if kind == "any":
        return pl.BlockSpec(memory_space=pl.ANY)
    if kind == "fixed":
        return pl.BlockSpec(shape, lambda n, info: (0,) + tail)
    if kind == "panel":
        return pl.BlockSpec(block, lambda n, info: (n + start,) + tail)
    if kind == "local":
        return pl.BlockSpec(block, lambda n, info: (n,) + tail)
    if kind in ("up", "down"):
        which = int(kind == "down")
        block = (shape[0], 1, 1) + tuple(shape[3:])
        return pl.BlockSpec(block, lambda n, info: (0, info[ORDER + n + start], which, 0, 0))
    if kind == "mine":
        return pl.BlockSpec(block, lambda n, info: (jnp.minimum(n, 1),) + tail)
    return pl.BlockSpec(block, lambda n, info: (jnp.maximum(n - 2, 0),) + tail)


def call(kernel, info, ins, outs, scratch=(), units=0, steps=PANELS, start=0, vmem="back"):
    moved = sum(a.size * a.dtype.itemsize for a, _ in ins)
    return pl.pallas_call(
        kernel,
        grid_spec=pltpu.PrefetchScalarGridSpec(
            num_scalar_prefetch=1,
            grid=(steps,),
            in_specs=[spec(a.shape, k, start) for a, k in ins],
            out_specs=[spec(s, k, start) for s, _, k in outs],
            scratch_shapes=list(scratch),
        ),
        out_shape=[jax.ShapeDtypeStruct(s, d) for s, d, _ in outs],
        compiler_params=pltpu.CompilerParams(vmem_limit_bytes=VMEM[vmem] << 20),
        cost_estimate=pl.CostEstimate(
            flops=int(2 * ROWS * D * D * units * steps), bytes_accessed=int(moved * 2), transcendentals=0
        ),
    )(info, *[a for a, _ in ins])


CORE, LINE_Y, LINE_X, NEAR_Z, FAR_Z = 1, 2, 4, 8, 16


def make_swap(devices):
    def swap(value, bit):
        return lax.ppermute(value, ("wide", "narrow"), [(i, i ^ bit) for i in range(devices)])

    return swap


def after(value, *others):
    return lax.optimization_barrier((value,) + others)[0] if others else value


class Gather:
    def __init__(self, swap, own):
        self.swap, self.own = swap, own

    def far(self, *wait):
        own = after(self.own, *wait)
        self.b0 = jnp.stack([own, self.swap(own, FAR_Z)])

    def near(self, *wait):
        self.b1 = self.swap(after(self.b0, *wait), NEAR_Z)

    def planes0(self, *wait):
        b0 = after(self.b0, *wait)
        self.x0, self.y0 = self.swap(b0, LINE_X), self.swap(b0, LINE_Y)

    def planes1(self, *wait):
        b1 = after(self.b1, *wait)
        self.x1, self.y1 = self.swap(b1, LINE_X), self.swap(b1, LINE_Y)

    def corners(self, *wait):
        x0, y1 = after(self.x0, *wait), after(self.y1, *wait)
        self.d0, self.d1 = self.swap(x0, LINE_Y), self.swap(y1, LINE_X)

    def mine(self):
        return [self.b0, self.b1, self.x0, self.x1, self.y0, self.y1, self.d0, self.d1]

    def theirs(self):
        return [self.swap(v, CORE) for v in self.mine()]


def merge_kernel(own_ref, *refs):
    got_refs, (keep_a, send_a, keep_b, send_b) = refs[:-4], refs[-4:]
    y, k = pl.program_id(0), pl.program_id(1)
    got = got_refs[0][...]
    if len(got_refs) == 2:
        got = jnp.where(y == 0, got, got_refs[1][...])
    value = (own_ref[...].astype(F32) + got.astype(F32)).astype(BF)

    @pl.when(k == 0)
    def _():
        keep_a[...] = value

    @pl.when(k == 1)
    def _():
        send_a[...] = value

    @pl.when((k >= 2) & (y == 0))
    def _():
        keep_b[...] = value

    @pl.when((k >= 2) & (y == 1))
    def _():
        send_b[...] = value


def merge(own, *got):
    rows = own.shape[2]
    block = (1, 2, rows, D)
    taken = pl.BlockSpec(block, lambda y, k: (y, k, 0, 0))
    by_y = pl.BlockSpec(block, lambda y, k: (y, 0, 0, 0))
    first = pl.BlockSpec(block, lambda y, k: (jnp.where(y == 0, jnp.maximum(k - 2, 0), 1), 0, 0, 0))
    second = pl.BlockSpec(block, lambda y, k: (jnp.where(y == 0, 0, jnp.maximum(k - 2, 0)), 0, 0, 0))
    size = own.size * 2
    gots = [taken]
    if len(got) == 2:
        gots = [
            pl.BlockSpec(block, lambda y, k: (0, jnp.where(y == 0, k, 3), 0, 0)),
            pl.BlockSpec(block, lambda y, k: (0, jnp.where(y == 0, 0, k), 0, 0)),
        ]
    return pl.pallas_call(
        merge_kernel,
        grid=(2, 4),
        in_specs=[taken] + gots,
        out_specs=[by_y, by_y, first, second],
        out_shape=[jax.ShapeDtypeStruct((2, 2, rows, D), BF)] * 4,
        compiler_params=pltpu.CompilerParams(vmem_limit_bytes=VMEM["merge"] << 20),
        cost_estimate=pl.CostEstimate(flops=0, bytes_accessed=3 * size, transcendentals=0),
    )(own, *got)


def total(*parts):
    value = parts[0].astype(F32)
    for p in parts[1:]:
        value = value + p.astype(F32)
    return value


class Scatter:
    def __init__(self, swap, *other):
        self.swap, self.state = swap, 0
        self.flight = tuple(swap(v, CORE) for v in other)

    def step(self, *wait, own=None):
        swap = self.swap
        got = tuple(after(f, *wait) for f in self.flight)
        self.state += 1
        if self.state == 1:
            self.a, send_a, self.b, send_b = merge(own, *got)
            self.flight = swap(send_a, LINE_X), swap(send_b, LINE_Y)
            return (send_a, send_b)
        if self.state == 2:
            send_a = total(self.a[1], got[0][1]).astype(BF)
            send_b = total(self.b[1], got[1][1]).astype(BF)
            self.a, self.b = (self.a[0], got[0][0]), (self.b[0], got[1][0])
            self.flight = swap(send_a, LINE_Y), swap(send_b, LINE_X)
            return (send_a, send_b)
        if self.state == 3:
            self.a = self.a + (got[0],)
            send = total(*self.b, got[1]).astype(BF)
            self.flight = (swap(send, NEAR_Z),)
            return (send,)
        if self.state == 4:
            self.a = self.a + (got[0],)
            send = total(*(p[1] for p in self.a)).astype(BF)
            self.flight = (swap(send, FAR_Z),)
            return (send,)
        self.result = total(*(p[0] for p in self.a), got[0])
        return (self.result,)


def body(
    tokens_in,
    cotangent,
    norm1_gain,
    norm1_shift,
    w_query,
    w_key,
    w_value,
    w_out,
    norm2_gain,
    norm2_shift,
    w_up,
    up_bias,
    w_down,
    down_bias,
    *,
    wide,
    narrow,
):
    direct = wide == 8 and narrow == 4
    wi, ni = lax.axis_index("wide"), lax.axis_index("narrow")
    swap = make_swap(wide * narrow)
    flipped = jnp.array([0, 2, 1, 3], jnp.int32)
    places = jnp.arange(PANELS, dtype=jnp.int32)
    back = flipped[jnp.bitwise_xor(ni, places)] if direct else places
    order = jnp.bitwise_xor(ni, flipped) if direct else places
    me = wi if direct else jnp.zeros_like(wi)
    info = jnp.concatenate(
        [v.astype(jnp.int32) for v in (me.reshape(1), (ni % 2).reshape(1), back, order)]
    )
    count, rows = tokens_in.shape[0], w_up.shape[0]
    vecs = jnp.stack([norm1_gain, norm1_shift, norm2_gain, norm2_shift, down_bias] + [down_bias] * 3)
    wide_row, turned = pltpu.VMEM((ROWS, D), F32), pltpu.VMEM((D, ROWS), BF)
    tokens32, tokens16 = ((ROWS, D), F32, "fixed"), ((ROWS, D), BF, "fixed")
    result32 = ((count, D), F32, "fixed")
    sums = ((8, D), F32, "fixed")
    blocks = 8 if direct else 1
    grads_a, grads_m = (2, blocks, D // blocks, D), (2, blocks, 2 * D // blocks, D)

    mlp = jnp.concatenate([w_up, w_down.T])
    if direct:
        full = lax.all_gather(mlp, ("wide", "narrow"), axis=0, tiled=False)
        full = full.reshape(wide, narrow, 2, rows, D)
    (attn,) = pl.pallas_call(
        pack_kernel,
        out_shape=[jax.ShapeDtypeStruct((rows, D), BF)],
        compiler_params=pltpu.CompilerParams(vmem_limit_bytes=VMEM["pack"] << 20),
    )(w_query, w_key, w_value, w_out)
    shared = jnp.where(ni % 2 == 1, tokens_in[:HALF], tokens_in[count - HALF :])
    shared = swap(shared, CORE)
    x, c, cb, h1 = call(
        prep_kernel,
        info,
        [(tokens_in, "fixed"), (cotangent, "fixed"), (shared, "fixed"), (vecs, "fixed")],
        [tokens32, tokens32, tokens16, ((ROWS + HALF_ROWS, D), BF, "fixed")],
        [pltpu.VMEM((HALF_ROWS, D), F32)],
        steps=1,
        vmem="prep",
    )
    if direct:
        ga = Gather(swap, attn)
        ga.far()
        ga.near()
        ga.planes0()
        ga.planes1(h1)
        ga.corners()
        sources = ga.mine() + ga.theirs()
        b_y, b_c = swap(after(up_bias, ga.d0, ga.d1), LINE_Y), swap(up_bias, CORE)
    else:

        def whole(v):
            return lax.all_gather(v, "narrow", axis=0, tiled=False)

        sources = [whole(lax.all_gather(attn, "wide", axis=0, tiled=True))]
        full = lax.all_gather(mlp.reshape(2, rows, D), "wide", axis=1, tiled=True)
        full = whole(full)[None]
        biases = whole(up_bias)
    qkv, o, a, y, h2 = call(
        functools.partial(forward_kernel, len(sources)),
        info,
        [(h1, "fixed"), (x, "fixed"), (vecs, "fixed")] + [(v, "any") for v in sources],
        [((PANELS, ROWS + HALF_ROWS, D), BF, "panel"), ((PANELS, ROWS, 256), BF, "panel")]
        + [((PANELS, D, D), BF, "panel"), tokens32, tokens16],
        [pltpu.VMEM((PANELS, D, D), BF), pltpu.SemaphoreType.DMA((PANELS, 8))],
        units=2,
        vmem="forward",
    )

    if direct:
        b_y = after(b_y, h2)
        biases = jnp.stack([up_bias, b_y, b_c, swap(b_y, CORE)])
    biases = biases.reshape(PANELS, 1, D)

    def mlp_part(start, more_in, more_out, more_scratch):
        return call(
            functools.partial(mlp_kernel, not start),
            info,
            [(h2, "fixed"), (cb, "fixed"), (biases, "panel"), (full, "up"), (full, "down")] + more_in,
            [((2, ROWS, D), BF, "local"), (grads_m, BF, "local"), ((2, 1, D), F32, "local")] + more_out,
            [turned, turned, pltpu.VMEM((ROWS, D), BF)] + more_scratch,
            units=5,
            steps=2,
            start=start,
            vmem="mlp",
        )

    act_t, dm_t, db_t, acc = mlp_part(2, [], [tokens32], [])
    if direct:
        sm = Scatter(swap, dm_t)
    act_m, dm_m, db_m, dy, dz, sums2 = mlp_part(
        0,
        [(acc, "fixed"), (c, "fixed"), (y, "fixed"), (vecs, "fixed")],
        [tokens32, tokens16, sums],
        [wide_row],
    )
    dzo = swap(dz[HALF_AT:], CORE)
    if direct:
        dz = after(dz, *sm.step(dz, own=dm_m))

    grads_one = ((1,) + grads_a[1:], BF, "fixed")
    da_m, *da_t, dq = call(
        back_kernel,
        info,
        [(dz, "fixed"), (dzo, "fixed"), (h1, "fixed"), (qkv, "panel"), (o, "panel"), (a, "panel")],
        [(grads_a, BF, "mine"), grads_one, grads_one, ((PANELS, ROWS, D), BF, "panel")],
        [turned, turned, pltpu.VMEM((ROWS + HALF_ROWS, 256), BF)],
        units=4,
    )
    if direct:
        sa = Scatter(swap, *da_t)
        sent = sm.step(dq)
        dq = after(dq, *sent, *sa.step(*sent, own=da_m))
    out, grad_x, small = call(
        late_kernel,
        info,
        [(dq, "panel"), (a, "panel"), (act_m, "mine"), (act_t, "theirs")]
        + [(full, "down"), (x, "fixed"), (y, "fixed"), (dy, "fixed")]
        + [(vecs, "fixed"), (sums2, "fixed"), (db_m, "fixed"), (db_t, "fixed")],
        [result32, result32, ((16, D), F32, "fixed")],
        [wide_row, wide_row, pltpu.VMEM((ROWS, D), BF)],
        units=2,
        vmem="late",
    )
    if direct:

        def reduced(small, bit, *wait):
            small = after(small, *wait)
            return small + swap(small, bit)

        wait = sa.step(small)
        small = reduced(reduced(small, CORE, *wait), FAR_Z)
        wait = sm.step(small)
        small = reduced(small, LINE_X, *sa.step(small, *wait))
        wait = sm.step(small)
        small = reduced(reduced(small, LINE_Y, *sa.step(small, *wait)), NEAR_Z)
        sm.step(), sa.step()
        grad_a, grad_u, grad_d = sa.result, sm.result[:rows], sm.result[rows:]
    else:

        def shard(own, other):
            v = jnp.concatenate([own, other]).reshape(PANELS, -1, D, D).astype(F32)
            v = lax.psum_scatter(v, "narrow", scatter_dimension=0, tiled=False)
            return lax.psum_scatter(v, "wide", scatter_dimension=1, tiled=True)

        (grad_a,), (grad_u, grad_d) = shard(da_m, jnp.concatenate(da_t)), shard(dm_m, dm_t)
        small = lax.psum(small, ("wide", "narrow"))
    pick_lanes = lambda low, high: jnp.concatenate(
        [grad_a[:, low : low + 128], grad_a[:, high : high + 64]], axis=1
    )
    return (
        out,
        grad_x,
        small[0],
        small[1],
        pick_lanes(0, 512),
        pick_lanes(128, 640),
        pick_lanes(256, 576),
        pick_lanes(384, 704).T,
        small[2],
        small[3],
        grad_u,
        lax.dynamic_index_in_dim(small, 5 + ni, 0, keepdims=False),
        grad_d.T,
        small[4],
    )


def solution(mesh):
    rows, cols, copied = P("wide", "narrow"), P("narrow", "wide"), P()
    tokens = P(("wide", "narrow"), None)
    return jax.shard_map(
        functools.partial(body, wide=mesh.shape["wide"], narrow=mesh.shape["narrow"]),
        mesh=mesh,
        in_specs=(tokens, tokens, copied, copied, rows, rows, rows, cols)
        + (copied, copied, rows, P("narrow"), cols, copied),
        out_specs=(tokens, tokens, copied, copied, rows, rows, rows, cols)
        + (copied, copied, rows, P("narrow"), cols, copied),
        check_vma=False,
    )
```

```python
import functools

import jax
import jax.numpy as jnp
from jax import lax
from jax.experimental import pallas as pl
from jax.experimental.pallas import tpu as pltpu
from jax.sharding import PartitionSpec as P

HEAD_DIM = 64
PATCHES = 196
EPS = 1e-06
D = 768
ROWS = 512
BLOCK = 208
FRAMES_AT = (0, 208)
HALF_AT = 400
HALF_ROWS = 112
HALF = PATCHES // 2
HALF_FIRST = 4
SCALE = HEAD_DIM ** (-0.5)
NEG = -1e30
VMEM = {"pack": 4, "prep": 8, "forward": 16, "mlp": 16, "back": 16, "late": 16, "merge": 8}
BF = jnp.bfloat16
F32 = jnp.float32


def nn(left, right):
    return jnp.dot(left, right, preferred_element_type=F32)


def nt(left, right):
    return lax.dot_general(left, right, (((1,), (1,)), ((), ())), preferred_element_type=F32)


def tn(left, right):
    return lax.dot_general(left, right, (((0,), (0,)), ((), ())), preferred_element_type=F32)


def lanes_below(shape, bound):
    return lax.broadcasted_iota(jnp.int32, shape, 1) < bound


def ln_stats(value):
    mean = jnp.mean(value, axis=1, keepdims=True)
    centred = value - mean
    rstd = lax.rsqrt(jnp.mean(centred * centred, axis=1, keepdims=True) + EPS)
    return centred * rstd, rstd


def ln_back(grad, normed, rstd, gain):
    scaled = grad * gain
    first = jnp.mean(scaled, axis=1, keepdims=True)
    second = jnp.mean(scaled * normed, axis=1, keepdims=True)
    return rstd * (scaled - first - normed * second)


def split(block):
    return (
        block[:, 0:128],
        block[:, 128:256],
        block[:, 256:384],
        block[:, 512:640],
        block[:, 640:768],
    )


def masked_pair(pair, low):
    zero = jnp.zeros_like(pair)
    return jnp.where(low, pair, zero), jnp.where(low, zero, pair)


def attend(queries, keys, valid):
    q01, qv2 = queries
    k01, v01, kv2, ko2 = keys
    low = lanes_below(q01.shape, 64)
    q0, q1 = masked_pair(q01, low)
    q2 = jnp.where(low, qv2, jnp.zeros_like(qv2))

    def probs(q, k):
        s = jnp.where(valid, nt(q, k) * SCALE, NEG)
        e = jnp.exp(s - jnp.max(s, axis=1, keepdims=True))
        return (e / jnp.sum(e, axis=1, keepdims=True)).astype(BF)

    o0 = nn(probs(q0, k01), v01)
    o1 = nn(probs(q1, k01), v01)
    o2 = nn(probs(q2, ko2), kv2)
    return jnp.concatenate(
        [jnp.where(low, o0, o1), jnp.where(low, 0.0, o2)], axis=1
    ).astype(BF)


def attend_back(queries, keys, dob, valid, own):
    q01, qv2 = queries
    k01, v01, kv2, ko2 = keys
    low = lanes_below(q01.shape, 64)
    d01, d2 = dob[:, 0:128], dob[:, 128:256]
    d2 = jnp.where(low, jnp.zeros_like(d2), d2)
    q0, q1 = masked_pair(q01, low)
    d0, d1 = masked_pair(d01, low)
    q2 = jnp.where(low, qv2, jnp.zeros_like(qv2))

    def one(q, k, d, v):
        st = jnp.where(valid, nt(k, q) * SCALE, NEG)
        e = jnp.exp(st - jnp.max(st, axis=0, keepdims=True))
        p = e / jnp.sum(e, axis=0, keepdims=True)
        dp = nt(v, d)
        ds = p * (dp - jnp.sum(p * dp, axis=0, keepdims=True))
        return p.astype(BF), ds.astype(BF)

    p0, s0 = one(q0, k01, d0, v01)
    p1, s1 = one(q1, k01, d1, v01)
    p2, s2 = one(q2, ko2, d2, kv2)
    low = low[:own]
    dq01 = jnp.where(low, tn(s0, k01)[:own], tn(s1, k01)[:own]) * SCALE
    dk01 = jnp.where(low, nn(s0[:own], q01), nn(s1[:own], q01)) * SCALE
    dv01 = jnp.where(low, nn(p0[:own], d01), nn(p1[:own], d01))
    dq2 = tn(s2, ko2)[:own] * SCALE
    dk2 = nn(s2[:own], qv2) * SCALE
    dv2 = nn(p2[:own], d2)
    rest = jnp.zeros_like(dq01)
    return jnp.concatenate(
        [dq01, dk01, dv01, rest, jnp.where(low, dq2, dv2), jnp.where(low, dk2, 0.0)], axis=1
    ).astype(BF)


def half_place(shape, axis):
    at = lax.broadcasted_iota(jnp.int32, shape, axis)
    at = jnp.where(at >= HALF_ROWS, at - HALF_ROWS, at)
    return (at >= HALF_FIRST) & (at < HALF_FIRST + HALF)


def pick(mine_ref, theirs_ref, into):
    n = pl.program_id(0)

    @pl.when(n < 2)
    def _():
        into[...] = mine_ref[0]

    @pl.when(n >= 2)
    def _():
        into[...] = theirs_ref[0]


def panel_copies(info_ref, sources, into, sem, start, p):
    if len(sources) == 1:
        return [pltpu.make_async_copy(sources[0].at[start + p], into.at[p], sem.at[p, 0])]
    copies = []
    for k in range(4):
        piece = sources[4 * p + k]
        rows = piece.shape[1]
        x, near = k // 2, k % 2
        for far in range(2):
            w = jnp.bitwise_xor(info_ref[WIDE], 2 * (2 * far + near) + x)
            at = pl.ds(pl.multiple_of(w * rows, rows), rows)
            copies.append(pltpu.make_async_copy(piece.at[far], into.at[p, at], sem.at[p, 2 * k + far]))
    return copies


def bring(info_ref, sources, into, sem, start, steps):
    n = pl.program_id(0)

    @pl.when(n == 0)
    def _():
        for p in range(steps):
            for c in panel_copies(info_ref, sources, into, sem, start, p):
                c.start()

    for p in range(steps):

        @pl.when(n == p)
        def _():
            for c in panel_copies(info_ref, sources, into, sem, start, p):
                c.wait()


def pack_kernel(wq_ref, wk_ref, wv_ref, wo_ref, attn_ref):
    size = wo_ref.shape[0]
    at = lax.broadcasted_iota(jnp.int32, (size, size), 0)
    eye = (at == lax.broadcasted_iota(jnp.int32, (size, size), 1)).astype(BF)
    wo = tn(wo_ref[...], eye).astype(BF)
    attn_ref[:, 0:128] = wq_ref[:, :128]
    attn_ref[:, 128:256] = wk_ref[:, :128]
    attn_ref[:, 256:384] = wv_ref[:, :128]
    attn_ref[:, 384:512] = wo[:, :128]
    attn_ref[:, 512:640] = jnp.concatenate([wq_ref[:, 128:], wv_ref[:, 128:]], axis=1)
    attn_ref[:, 640:768] = jnp.concatenate([wk_ref[:, 128:], wo[:, 128:]], axis=1)


def spread(into, value, odd):
    zero = jnp.zeros_like(value)
    into[PATCHES:BLOCK] = zero[: BLOCK - PATCHES]
    end = HALF_AT + HALF_FIRST + HALF
    into[end:] = zero[: ROWS - end]

    @pl.when(odd == 0)
    def _():
        into[:PATCHES] = value[:PATCHES]
        into[BLOCK:end] = value[PATCHES:]

    @pl.when(odd == 1)
    def _():
        into[:PATCHES] = value[HALF : HALF + PATCHES]
        into[BLOCK : BLOCK + PATCHES] = value[HALF + PATCHES :]
        into[BLOCK + PATCHES : end] = value[:HALF]


def gather_back(into, value, odd):
    end = HALF_AT + HALF_FIRST + HALF

    @pl.when(odd == 0)
    def _():
        into[:PATCHES] = value[:PATCHES]
        into[PATCHES:] = value[BLOCK:end]

    @pl.when(odd == 1)
    def _():
        into[:HALF] = value[BLOCK + PATCHES : end]
        into[HALF : HALF + PATCHES] = value[:PATCHES]
        into[HALF + PATCHES :] = value[BLOCK : BLOCK + PATCHES]


def prep_kernel(info_ref, x_ref, c_ref, xo_ref, vec_ref, xp_ref, cp_ref, cb_ref, h_ref, other):
    odd = info_ref[ODD]
    gain, shift = vec_ref[0:1, :], vec_ref[1:2, :]
    spread(xp_ref, x_ref[...].astype(F32), odd)
    spread(cp_ref, c_ref[...], odd)
    cb_ref[...] = cp_ref[...].astype(BF)
    normed, _ = ln_stats(xp_ref[...])
    h_ref[:ROWS] = (normed * gain + shift).astype(BF)
    other[...] = jnp.zeros_like(other)
    other[HALF_FIRST : HALF_FIRST + HALF] = xo_ref[...].astype(F32)
    normed, _ = ln_stats(other[...])
    h_ref[ROWS:] = (normed * gain + shift).astype(BF)


def forward_kernel(pieces, info_ref, h_ref, x_ref, vec_ref, *refs):
    sources, refs = refs[:pieces], refs[pieces:]
    qkv_ref, o_ref, a_ref, y_ref, h2_ref, w, sem = refs
    n = pl.program_id(0)
    bring(info_ref, sources, w, sem, 0, PANELS)
    a_ref[0] = w[n]
    qkv_ref[0] = nn(h_ref[...], w[n]).astype(BF)
    valid = lanes_below((BLOCK, BLOCK), PATCHES)
    for at in FRAMES_AT:
        q01, k01, v01, qv2, ko2 = split(qkv_ref[0, at : at + BLOCK, :])
        o_ref[0, at : at + BLOCK, :] = attend((q01, qv2), (k01, v01, qv2, ko2), valid)
    q01, k01, v01, qv2, ko2 = split(qkv_ref[0, HALF_AT:, :])
    valid = half_place((HALF_ROWS, 2 * HALF_ROWS), 1)
    part = attend((q01[:HALF_ROWS], qv2[:HALF_ROWS]), (k01, v01, qv2, ko2), valid)
    first = lax.broadcasted_iota(jnp.int32, (16, 256), 0) < HALF_FIRST
    o_ref[0, HALF_AT : HALF_AT + 16] = jnp.where(first, o_ref[0, HALF_AT : HALF_AT + 16], part[:16])
    o_ref[0, HALF_AT + 16 :] = part[16:]
    o = o_ref[0]
    z = nt(o[:, :128], a_ref[0, :, 384:512]) + nt(o[:, 128:], a_ref[0, :, 640:768])

    @pl.when(n == 0)
    def _():
        y_ref[...] = x_ref[...] + z

    @pl.when(n > 0)
    def _():
        y_ref[...] += z

    @pl.when(n == PANELS - 1)
    def _():
        normed, _ = ln_stats(y_ref[...])
        h2_ref[...] = (normed * vec_ref[2:3, :] + vec_ref[3:4, :]).astype(BF)


def store_blocks(out_ref, value, me, part=0):
    blocks = out_ref.shape[1]
    rows = value.shape[0] // blocks
    value = value.astype(BF)
    for w in range(blocks):
        if blocks == 1:
            place = 0
        else:
            r = jnp.bitwise_xor(w, me)
            place = (r & 2) * 2 + (r & 1) * 2 + lax.shift_right_logical(r, 2)
        out_ref[0, place, part * rows : (part + 1) * rows] = value[w * rows : (w + 1) * rows]


def mlp_kernel(last, info_ref, h_ref, cb_ref, b_ref, u_ref, d_ref, *refs):
    if last:
        base_ref, c_ref, y_ref, vec_ref, act_ref, dm_ref, db_ref, dy_ref, dz_ref, sums_ref, *refs = refs
        ht, ct, dub, acc = refs
    else:
        act_ref, dm_ref, db_ref, acc, ht, ct, dub = refs
    n = pl.program_id(0)

    @pl.when(n == 0)
    def _():
        ht[...] = h_ref[...].T
        ct[...] = cb_ref[...].T

    for j in range(3):
        cols = slice(256 * j, 256 * j + 256)
        up = u_ref[:, 0, 0, :, cols].reshape(D, 256)
        down = d_ref[:, 0, 0, :, cols].reshape(D, 256)
        u = nn(h_ref[...], up) + b_ref[0, :, cols]
        big = 0.5 * (1.0 + lax.erf(u * (0.5**0.5)))
        small = jnp.exp(-0.5 * u * u) * 0.3989422804014327
        act_ref[0, :, cols] = (u * big).astype(BF)
        du = nn(cb_ref[...], down) * (big + u * small)
        db_ref[0, :, cols] = jnp.sum(du, axis=0, keepdims=True)
        dub[:, cols] = du.astype(BF)
    dh = nt(dub[...], u_ref[...].reshape(D, D))
    store_blocks(dm_ref, nn(ht[...], dub[...]), info_ref[WIDE], 0)
    store_blocks(dm_ref, nn(ct[...], act_ref[0]), info_ref[WIDE], 1)

    @pl.when(n == 0)
    def _():
        acc[...] = base_ref[...] + dh if last else dh

    @pl.when(n == 1)
    def _():
        acc[...] += dh
        if last:
            normed, rstd = ln_stats(y_ref[...])
            grad = acc[...]
            c = c_ref[...]
            dy = c + ln_back(grad, normed, rstd, vec_ref[2:3, :])
            dy_ref[...] = dy
            dz_ref[...] = dy.astype(BF)
            sums_ref[0:1, :] = jnp.sum(grad * normed, axis=0, keepdims=True)
            sums_ref[1:2, :] = jnp.sum(grad, axis=0, keepdims=True)
            sums_ref[2:3, :] = jnp.sum(c, axis=0, keepdims=True)


def back_kernel(info_ref, dz_ref, dzo_ref, h_ref, qkv_ref, o_ref, a_ref, dam_ref, dat0_ref, dat1_ref, dq_ref, ht, dt, dob):
    n = pl.program_id(0)

    @pl.when(n == 0)
    def _():
        ht[...] = h_ref[:ROWS].T
        dt[...] = dz_ref[...].T

    for into, cols in ((0, 384), (128, 640)):
        weight = a_ref[0, :, cols : cols + 128]
        dob[:ROWS, into : into + 128] = nn(dz_ref[...], weight).astype(BF)
        dob[ROWS:, into : into + 128] = nn(dzo_ref[...], weight).astype(BF)
    valid = lax.broadcasted_iota(jnp.int32, (BLOCK, BLOCK), 0) < PATCHES
    for at in FRAMES_AT:
        q01, k01, v01, qv2, ko2 = split(qkv_ref[0, at : at + BLOCK, :])
        d = dob[at : at + BLOCK]
        inside = lax.broadcasted_iota(jnp.int32, d.shape, 0) < PATCHES
        d = jnp.where(inside, d, jnp.zeros_like(d))
        dq_ref[0, at : at + BLOCK] = attend_back(
            (q01, qv2), (k01, v01, qv2, ko2), d, valid, BLOCK
        )
    q01, k01, v01, qv2, ko2 = split(qkv_ref[0, HALF_AT:, :])
    d = dob[HALF_AT:]
    d = jnp.where(half_place(d.shape, 0), d, jnp.zeros_like(d))
    valid = half_place((2 * HALF_ROWS, 2 * HALF_ROWS), 0)
    part = attend_back((q01, qv2), (k01, v01, qv2, ko2), d, valid, HALF_ROWS)
    first = lax.broadcasted_iota(jnp.int32, (16, D), 0) < HALF_FIRST
    dq_ref[0, HALF_AT : HALF_AT + 16] = jnp.where(first, dq_ref[0, HALF_AT : HALF_AT + 16], part[:16])
    dq_ref[0, HALF_AT + 16 :] = part[16:]
    left = nn(ht[...], dq_ref[0, :, 0:384])
    right = nn(ht[...], dq_ref[0, :, 512:768])
    outs = nn(dt[...], o_ref[0])
    value = jnp.concatenate(
        [left, outs[:, 0:128], right[:, 0:128], right[:, 128:256] + outs[:, 128:256]], axis=1
    )

    @pl.when(n < 2)
    def _():
        store_blocks(dam_ref, value, info_ref[WIDE])

    @pl.when(n == 2)
    def _():
        store_blocks(dat0_ref, value, info_ref[WIDE])

    @pl.when(n == 3)
    def _():
        store_blocks(dat1_ref, value, info_ref[WIDE])


def late_kernel(
    info_ref,
    dq_ref,
    a_ref,
    actm_ref,
    actt_ref,
    d_ref,
    x_ref,
    y_ref,
    dy_ref,
    vec_ref,
    sums_ref,
    dbm_ref,
    dbt_ref,
    out_ref,
    grad_ref,
    small_ref,
    acc,
    acc2,
    left,
):
    n = pl.program_id(0)
    dh = nt(dq_ref[0], a_ref[0])

    @pl.when(n == 0)
    def _():
        acc[...] = dh

    @pl.when(n > 0)
    def _():
        acc[...] += dh

    pick(actm_ref, actt_ref, left)
    y2 = nt(left[...], d_ref[...].reshape(D, D))

    @pl.when(n == 0)
    def _():
        acc2[...] = y_ref[...] + y2 + vec_ref[4:5, :]

    @pl.when(n > 0)
    def _():
        acc2[...] += y2

    @pl.when(n == pl.num_programs(0) - 1)
    def _():
        normed, rstd = ln_stats(x_ref[...])
        grad = acc[...]
        small_ref[0:1, :] = jnp.sum(grad * normed, axis=0, keepdims=True)
        small_ref[1:2, :] = jnp.sum(grad, axis=0, keepdims=True)
        small_ref[2:5, :] = sums_ref[0:3, :]
        for j in range(PANELS):
            at = info_ref[BACK + j]

            @pl.when(at < 2)
            def _():
                small_ref[5 + j : 6 + j, :] = dbm_ref[at]

            @pl.when(at >= 2)
            def _():
                small_ref[5 + j : 6 + j, :] = dbt_ref[at - 2]

        gather_back(grad_ref, dy_ref[...] + ln_back(grad, normed, rstd, vec_ref[0:1, :]), info_ref[ODD])
        gather_back(out_ref, acc2[...], info_ref[ODD])


WIDE, ODD, BACK, ORDER = 0, 1, 2, 6
PANELS = 4


def spec(shape, kind, start):
    tail = (0,) * (len(shape) - 1)
    block = (1,) + tuple(shape[1:])
    if kind == "any":
        return pl.BlockSpec(memory_space=pl.ANY)
    if kind == "fixed":
        return pl.BlockSpec(shape, lambda n, info: (0,) + tail)
    if kind == "panel":
        return pl.BlockSpec(block, lambda n, info: (n + start,) + tail)
    if kind == "local":
        return pl.BlockSpec(block, lambda n, info: (n,) + tail)
    if kind in ("up", "down"):
        which = int(kind == "down")
        block = (shape[0], 1, 1) + tuple(shape[3:])
        return pl.BlockSpec(block, lambda n, info: (0, info[ORDER + n + start], which, 0, 0))
    if kind == "mine":
        return pl.BlockSpec(block, lambda n, info: (jnp.minimum(n, 1),) + tail)
    return pl.BlockSpec(block, lambda n, info: (jnp.maximum(n - 2, 0),) + tail)


def call(kernel, info, ins, outs, scratch=(), units=0, steps=PANELS, start=0, vmem="back"):
    moved = sum(a.size * a.dtype.itemsize for a, _ in ins)
    return pl.pallas_call(
        kernel,
        grid_spec=pltpu.PrefetchScalarGridSpec(
            num_scalar_prefetch=1,
            grid=(steps,),
            in_specs=[spec(a.shape, k, start) for a, k in ins],
            out_specs=[spec(s, k, start) for s, _, k in outs],
            scratch_shapes=list(scratch),
        ),
        out_shape=[jax.ShapeDtypeStruct(s, d) for s, d, _ in outs],
        compiler_params=pltpu.CompilerParams(vmem_limit_bytes=VMEM[vmem] << 20),
        cost_estimate=pl.CostEstimate(
            flops=int(2 * ROWS * D * D * units * steps), bytes_accessed=int(moved * 2), transcendentals=0
        ),
    )(info, *[a for a, _ in ins])


CORE, LINE_Y, LINE_X, NEAR_Z, FAR_Z = 1, 2, 4, 8, 16


def make_swap(devices):
    def swap(value, bit):
        return lax.ppermute(value, ("wide", "narrow"), [(i, i ^ bit) for i in range(devices)])

    return swap


def after(value, *others):
    return lax.optimization_barrier((value,) + others)[0] if others else value


class Gather:
    def __init__(self, swap, own):
        self.swap, self.own = swap, own

    def far(self, *wait):
        own = after(self.own, *wait)
        self.b0 = jnp.stack([own, self.swap(own, FAR_Z)])

    def near(self, *wait):
        self.b1 = self.swap(after(self.b0, *wait), NEAR_Z)

    def planes0(self, *wait):
        b0 = after(self.b0, *wait)
        self.x0, self.y0 = self.swap(b0, LINE_X), self.swap(b0, LINE_Y)

    def planes1(self, *wait):
        b1 = after(self.b1, *wait)
        self.x1, self.y1 = self.swap(b1, LINE_X), self.swap(b1, LINE_Y)

    def corners(self, *wait):
        x0, y1 = after(self.x0, *wait), after(self.y1, *wait)
        self.d0, self.d1 = self.swap(x0, LINE_Y), self.swap(y1, LINE_X)

    def mine(self):
        return [self.b0, self.b1, self.x0, self.x1, self.y0, self.y1, self.d0, self.d1]

    def theirs(self):
        return [self.swap(v, CORE) for v in self.mine()]


def merge_kernel(own_ref, *refs):
    got_refs, (keep_a, send_a, keep_b, send_b) = refs[:-4], refs[-4:]
    y, k = pl.program_id(0), pl.program_id(1)
    got = got_refs[0][...]
    if len(got_refs) == 2:
        got = jnp.where(y == 0, got, got_refs[1][...])
    value = (own_ref[...].astype(F32) + got.astype(F32)).astype(BF)

    @pl.when(k == 0)
    def _():
        keep_a[...] = value

    @pl.when(k == 1)
    def _():
        send_a[...] = value

    @pl.when((k >= 2) & (y == 0))
    def _():
        keep_b[...] = value

    @pl.when((k >= 2) & (y == 1))
    def _():
        send_b[...] = value


def merge(own, *got):
    rows = own.shape[2]
    block = (1, 2, rows, D)
    taken = pl.BlockSpec(block, lambda y, k: (y, k, 0, 0))
    by_y = pl.BlockSpec(block, lambda y, k: (y, 0, 0, 0))
    first = pl.BlockSpec(block, lambda y, k: (jnp.where(y == 0, jnp.maximum(k - 2, 0), 1), 0, 0, 0))
    second = pl.BlockSpec(block, lambda y, k: (jnp.where(y == 0, 0, jnp.maximum(k - 2, 0)), 0, 0, 0))
    size = own.size * 2
    gots = [taken]
    if len(got) == 2:
        gots = [
            pl.BlockSpec(block, lambda y, k: (0, jnp.where(y == 0, k, 3), 0, 0)),
            pl.BlockSpec(block, lambda y, k: (0, jnp.where(y == 0, 0, k), 0, 0)),
        ]
    return pl.pallas_call(
        merge_kernel,
        grid=(2, 4),
        in_specs=[taken] + gots,
        out_specs=[by_y, by_y, first, second],
        out_shape=[jax.ShapeDtypeStruct((2, 2, rows, D), BF)] * 4,
        compiler_params=pltpu.CompilerParams(vmem_limit_bytes=VMEM["merge"] << 20),
        cost_estimate=pl.CostEstimate(flops=0, bytes_accessed=3 * size, transcendentals=0),
    )(own, *got)


def total(*parts):
    value = parts[0].astype(F32)
    for p in parts[1:]:
        value = value + p.astype(F32)
    return value


class Scatter:
    def __init__(self, swap, *other):
        self.swap, self.state = swap, 0
        self.flight = tuple(swap(v, CORE) for v in other)

    def step(self, *wait, own=None):
        swap = self.swap
        got = lax.optimization_barrier(self.flight + wait)[: len(self.flight)]
        self.state += 1
        if self.state == 1:
            self.a, send_a, self.b, send_b = merge(own, *got)
            self.flight = swap(send_a, LINE_X), swap(send_b, LINE_Y)
            return (send_a, send_b)
        if self.state == 2:
            send_a = total(self.a[1], got[0][1]).astype(BF)
            send_b = total(self.b[1], got[1][1]).astype(BF)
            self.a, self.b = (self.a[0], got[0][0]), (self.b[0], got[1][0])
            self.flight = swap(send_a, LINE_Y), swap(send_b, LINE_X)
            return (send_a, send_b)
        if self.state == 3:
            self.a = self.a + (got[0],)
            send = total(*self.b, got[1]).astype(BF)
            self.flight = (swap(send, NEAR_Z),)
            return (send,)
        if self.state == 4:
            self.a = self.a + (got[0],)
            send = total(*(p[1] for p in self.a)).astype(BF)
            self.flight = (swap(send, FAR_Z),)
            return (send,)
        self.result = total(*(p[0] for p in self.a), got[0])
        return (self.result,)


def body(
    tokens_in,
    cotangent,
    norm1_gain,
    norm1_shift,
    w_query,
    w_key,
    w_value,
    w_out,
    norm2_gain,
    norm2_shift,
    w_up,
    up_bias,
    w_down,
    down_bias,
    *,
    wide,
    narrow,
):
    direct = wide == 8 and narrow == 4
    wi, ni = lax.axis_index("wide"), lax.axis_index("narrow")
    swap = make_swap(wide * narrow)
    flipped = jnp.array([0, 2, 1, 3], jnp.int32)
    places = jnp.arange(PANELS, dtype=jnp.int32)
    back = flipped[jnp.bitwise_xor(ni, places)] if direct else places
    order = jnp.bitwise_xor(ni, flipped) if direct else places
    me = wi if direct else jnp.zeros_like(wi)
    info = jnp.concatenate(
        [v.astype(jnp.int32) for v in (me.reshape(1), (ni % 2).reshape(1), back, order)]
    )
    count, rows = tokens_in.shape[0], w_up.shape[0]
    vecs = jnp.stack([norm1_gain, norm1_shift, norm2_gain, norm2_shift, down_bias] + [down_bias] * 3)
    wide_row, turned = pltpu.VMEM((ROWS, D), F32), pltpu.VMEM((D, ROWS), BF)
    tokens32, tokens16 = ((ROWS, D), F32, "fixed"), ((ROWS, D), BF, "fixed")
    result32 = ((count, D), F32, "fixed")
    sums = ((8, D), F32, "fixed")
    blocks = 8 if direct else 1
    grads_a, grads_m = (2, blocks, D // blocks, D), (2, blocks, 2 * D // blocks, D)

    mlp = jnp.concatenate([w_up, w_down.T])
    if direct:
        full = lax.all_gather(mlp, ("wide", "narrow"), axis=0, tiled=False)
        full = full.reshape(wide, narrow, 2, rows, D)
    (attn,) = pl.pallas_call(
        pack_kernel,
        out_shape=[jax.ShapeDtypeStruct((rows, D), BF)],
        compiler_params=pltpu.CompilerParams(vmem_limit_bytes=VMEM["pack"] << 20),
    )(w_query, w_key, w_value, w_out)
    shared = jnp.where(ni % 2 == 1, tokens_in[:HALF], tokens_in[count - HALF :])
    shared = swap(shared, CORE)
    x, c, cb, h1 = call(
        prep_kernel,
        info,
        [(tokens_in, "fixed"), (cotangent, "fixed"), (shared, "fixed"), (vecs, "fixed")],
        [tokens32, tokens32, tokens16, ((ROWS + HALF_ROWS, D), BF, "fixed")],
        [pltpu.VMEM((HALF_ROWS, D), F32)],
        steps=1,
        vmem="prep",
    )
    if direct:
        ga = Gather(swap, attn)
        ga.far()
        ga.near()
        ga.planes0()
        ga.planes1(h1)
        ga.corners()
        sources = ga.mine() + ga.theirs()
        b_y, b_c = swap(after(up_bias, ga.d0, ga.d1), LINE_Y), swap(up_bias, CORE)
    else:

        def whole(v):
            return lax.all_gather(v, "narrow", axis=0, tiled=False)

        sources = [whole(lax.all_gather(attn, "wide", axis=0, tiled=True))]
        full = lax.all_gather(mlp.reshape(2, rows, D), "wide", axis=1, tiled=True)
        full = whole(full)[None]
        biases = whole(up_bias)
    qkv, o, a, y, h2 = call(
        functools.partial(forward_kernel, len(sources)),
        info,
        [(h1, "fixed"), (x, "fixed"), (vecs, "fixed")] + [(v, "any") for v in sources],
        [((PANELS, ROWS + HALF_ROWS, D), BF, "panel"), ((PANELS, ROWS, 256), BF, "panel")]
        + [((PANELS, D, D), BF, "panel"), tokens32, tokens16],
        [pltpu.VMEM((PANELS, D, D), BF), pltpu.SemaphoreType.DMA((PANELS, 8))],
        units=2,
        vmem="forward",
    )

    if direct:
        b_y = after(b_y, h2)
        biases = jnp.stack([up_bias, b_y, b_c, swap(b_y, CORE)])
    biases = biases.reshape(PANELS, 1, D)

    def mlp_part(start, more_in, more_out, more_scratch):
        return call(
            functools.partial(mlp_kernel, not start),
            info,
            [(h2, "fixed"), (cb, "fixed"), (biases, "panel"), (full, "up"), (full, "down")] + more_in,
            [((2, ROWS, D), BF, "local"), (grads_m, BF, "local"), ((2, 1, D), F32, "local")] + more_out,
            [turned, turned, pltpu.VMEM((ROWS, D), BF)] + more_scratch,
            units=5,
            steps=2,
            start=start,
            vmem="mlp",
        )

    act_t, dm_t, db_t, acc = mlp_part(2, [], [tokens32], [])
    if direct:
        sm = Scatter(swap, dm_t)
    act_m, dm_m, db_m, dy, dz, sums2 = mlp_part(
        0,
        [(acc, "fixed"), (c, "fixed"), (y, "fixed"), (vecs, "fixed")],
        [tokens32, tokens16, sums],
        [wide_row],
    )
    dzo = swap(dz[HALF_AT:], CORE)
    if direct:
        dz = after(dz, *sm.step(dz, own=dm_m))

    grads_one = ((1,) + grads_a[1:], BF, "fixed")
    da_m, *da_t, dq = call(
        back_kernel,
        info,
        [(dz, "fixed"), (dzo, "fixed"), (h1, "fixed"), (qkv, "panel"), (o, "panel"), (a, "panel")],
        [(grads_a, BF, "mine"), grads_one, grads_one, ((PANELS, ROWS, D), BF, "panel")],
        [turned, turned, pltpu.VMEM((ROWS + HALF_ROWS, 256), BF)],
        units=4,
    )
    if direct:
        sa = Scatter(swap, *da_t)
        sent = sm.step(dq)
        dq = after(dq, *sent, *sa.step(*sent, own=da_m))
    out, grad_x, small = call(
        late_kernel,
        info,
        [(dq, "panel"), (a, "panel"), (act_m, "mine"), (act_t, "theirs")]
        + [(full, "down"), (x, "fixed"), (y, "fixed"), (dy, "fixed")]
        + [(vecs, "fixed"), (sums2, "fixed"), (db_m, "fixed"), (db_t, "fixed")],
        [result32, result32, ((16, D), F32, "fixed")],
        [wide_row, wide_row, pltpu.VMEM((ROWS, D), BF)],
        units=2,
        vmem="late",
    )
    if direct:

        def reduced(small, bit, *wait):
            small = after(small, *wait)
            return small + swap(small, bit)

        near = sm.step(small)
        small = reduced(reduced(small, CORE), LINE_X, *near)
        small = reduced(small, FAR_Z, *sa.step(small))
        far = sm.step()
        small = reduced(small, NEAR_Z, *sa.step(small, *far))
        small = reduced(small, LINE_Y, *sa.step(small, *sm.step()))
        sa.step()
        grad_a, grad_u, grad_d = sa.result, sm.result[:rows], sm.result[rows:]
    else:

        def shard(own, other):
            v = jnp.concatenate([own, other]).reshape(PANELS, -1, D, D).astype(F32)
            v = lax.psum_scatter(v, "narrow", scatter_dimension=0, tiled=False)
            return lax.psum_scatter(v, "wide", scatter_dimension=1, tiled=True)

        (grad_a,), (grad_u, grad_d) = shard(da_m, jnp.concatenate(da_t)), shard(dm_m, dm_t)
        small = lax.psum(small, ("wide", "narrow"))
    pick_lanes = lambda low, high: jnp.concatenate(
        [grad_a[:, low : low + 128], grad_a[:, high : high + 64]], axis=1
    )
    return (
        out,
        grad_x,
        small[0],
        small[1],
        pick_lanes(0, 512),
        pick_lanes(128, 640),
        pick_lanes(256, 576),
        pick_lanes(384, 704).T,
        small[2],
        small[3],
        grad_u,
        lax.dynamic_index_in_dim(small, 5 + ni, 0, keepdims=False),
        grad_d.T,
        small[4],
    )


def solution(mesh):
    rows, cols, copied = P("wide", "narrow"), P("narrow", "wide"), P()
    tokens = P(("wide", "narrow"), None)
    return jax.shard_map(
        functools.partial(body, wide=mesh.shape["wide"], narrow=mesh.shape["narrow"]),
        mesh=mesh,
        in_specs=(tokens, tokens, copied, copied, rows, rows, rows, cols)
        + (copied, copied, rows, P("narrow"), cols, copied),
        out_specs=(tokens, tokens, copied, copied, rows, rows, rows, cols)
        + (copied, copied, rows, P("narrow"), cols, copied),
        check_vma=False,
    )
```

```python
import functools

import jax
import jax.numpy as jnp
from jax import lax
from jax.experimental import pallas as pl
from jax.experimental.pallas import tpu as pltpu
from jax.sharding import PartitionSpec as P

HEAD_DIM = 64
PATCHES = 196
EPS = 1e-06
D = 768
ROWS = 512
BLOCK = 208
FRAMES_AT = (0, 208)
HALF_AT = 400
HALF_ROWS = 112
HALF = PATCHES // 2
HALF_FIRST = 4
SCALE = HEAD_DIM ** (-0.5)
NEG = -1e30
VMEM = {"pack": 4, "prep": 8, "forward": 16, "mlp": 16, "back": 16, "late": 16, "merge": 8}
BF = jnp.bfloat16
F32 = jnp.float32


def nn(left, right):
    return jnp.dot(left, right, preferred_element_type=F32)


def nt(left, right):
    return lax.dot_general(left, right, (((1,), (1,)), ((), ())), preferred_element_type=F32)


def tn(left, right):
    return lax.dot_general(left, right, (((0,), (0,)), ((), ())), preferred_element_type=F32)


def lanes_below(shape, bound):
    return lax.broadcasted_iota(jnp.int32, shape, 1) < bound


def ln_stats(value):
    mean = jnp.mean(value, axis=1, keepdims=True)
    centred = value - mean
    rstd = lax.rsqrt(jnp.mean(centred * centred, axis=1, keepdims=True) + EPS)
    return centred * rstd, rstd


def ln_back(grad, normed, rstd, gain):
    scaled = grad * gain
    first = jnp.mean(scaled, axis=1, keepdims=True)
    second = jnp.mean(scaled * normed, axis=1, keepdims=True)
    return rstd * (scaled - first - normed * second)


def split(block):
    return (
        block[:, 0:128],
        block[:, 128:256],
        block[:, 256:384],
        block[:, 512:640],
        block[:, 640:768],
    )


def masked_pair(pair, low):
    zero = jnp.zeros_like(pair)
    return jnp.where(low, pair, zero), jnp.where(low, zero, pair)


def attend(queries, keys, valid):
    q01, qv2 = queries
    k01, v01, kv2, ko2 = keys
    low = lanes_below(q01.shape, 64)
    q0, q1 = masked_pair(q01, low)
    q2 = jnp.where(low, qv2, jnp.zeros_like(qv2))

    def probs(q, k):
        s = jnp.where(valid, nt(q, k) * SCALE, NEG)
        e = jnp.exp(s - jnp.max(s, axis=1, keepdims=True))
        return (e / jnp.sum(e, axis=1, keepdims=True)).astype(BF)

    o0 = nn(probs(q0, k01), v01)
    o1 = nn(probs(q1, k01), v01)
    o2 = nn(probs(q2, ko2), kv2)
    return jnp.concatenate(
        [jnp.where(low, o0, o1), jnp.where(low, 0.0, o2)], axis=1
    ).astype(BF)


def attend_back(queries, keys, dob, valid, own):
    q01, qv2 = queries
    k01, v01, kv2, ko2 = keys
    low = lanes_below(q01.shape, 64)
    d01, d2 = dob[:, 0:128], dob[:, 128:256]
    d2 = jnp.where(low, jnp.zeros_like(d2), d2)
    q0, q1 = masked_pair(q01, low)
    d0, d1 = masked_pair(d01, low)
    q2 = jnp.where(low, qv2, jnp.zeros_like(qv2))

    def one(q, k, d, v):
        st = jnp.where(valid, nt(k, q) * SCALE, NEG)
        e = jnp.exp(st - jnp.max(st, axis=0, keepdims=True))
        p = e / jnp.sum(e, axis=0, keepdims=True)
        dp = nt(v, d)
        ds = p * (dp - jnp.sum(p * dp, axis=0, keepdims=True))
        return p.astype(BF), ds.astype(BF)

    p0, s0 = one(q0, k01, d0, v01)
    p1, s1 = one(q1, k01, d1, v01)
    p2, s2 = one(q2, ko2, d2, kv2)
    low = low[:own]
    dq01 = jnp.where(low, tn(s0, k01)[:own], tn(s1, k01)[:own]) * SCALE
    dk01 = jnp.where(low, nn(s0[:own], q01), nn(s1[:own], q01)) * SCALE
    dv01 = jnp.where(low, nn(p0[:own], d01), nn(p1[:own], d01))
    dq2 = tn(s2, ko2)[:own] * SCALE
    dk2 = nn(s2[:own], qv2) * SCALE
    dv2 = nn(p2[:own], d2)
    rest = jnp.zeros_like(dq01)
    return jnp.concatenate(
        [dq01, dk01, dv01, rest, jnp.where(low, dq2, dv2), jnp.where(low, dk2, 0.0)], axis=1
    ).astype(BF)


def half_place(shape, axis):
    at = lax.broadcasted_iota(jnp.int32, shape, axis)
    at = jnp.where(at >= HALF_ROWS, at - HALF_ROWS, at)
    return (at >= HALF_FIRST) & (at < HALF_FIRST + HALF)


def pick(mine_ref, theirs_ref, into):
    n = pl.program_id(0)

    @pl.when(n < 2)
    def _():
        into[...] = mine_ref[0]

    @pl.when(n >= 2)
    def _():
        into[...] = theirs_ref[0]


def panel_copies(info_ref, sources, into, sem, start, p):
    if len(sources) == 1:
        return [pltpu.make_async_copy(sources[0].at[start + p], into.at[p], sem.at[p, 0])]
    copies = []
    for k in range(4):
        piece = sources[4 * p + k]
        rows = piece.shape[1]
        x, near = k // 2, k % 2
        for far in range(2):
            w = jnp.bitwise_xor(info_ref[WIDE], 2 * (2 * far + near) + x)
            at = pl.ds(pl.multiple_of(w * rows, rows), rows)
            copies.append(pltpu.make_async_copy(piece.at[far], into.at[p, at], sem.at[p, 2 * k + far]))
    return copies


def bring(info_ref, sources, into, sem, start, steps):
    n = pl.program_id(0)

    @pl.when(n == 0)
    def _():
        for p in range(steps):
            for c in panel_copies(info_ref, sources, into, sem, start, p):
                c.start()

    for p in range(steps):

        @pl.when(n == p)
        def _():
            for c in panel_copies(info_ref, sources, into, sem, start, p):
                c.wait()


def pack_kernel(wq_ref, wk_ref, wv_ref, wo_ref, attn_ref):
    size = wo_ref.shape[0]
    at = lax.broadcasted_iota(jnp.int32, (size, size), 0)
    eye = (at == lax.broadcasted_iota(jnp.int32, (size, size), 1)).astype(BF)
    wo = tn(wo_ref[...], eye).astype(BF)
    attn_ref[:, 0:128] = wq_ref[:, :128]
    attn_ref[:, 128:256] = wk_ref[:, :128]
    attn_ref[:, 256:384] = wv_ref[:, :128]
    attn_ref[:, 384:512] = wo[:, :128]
    attn_ref[:, 512:640] = jnp.concatenate([wq_ref[:, 128:], wv_ref[:, 128:]], axis=1)
    attn_ref[:, 640:768] = jnp.concatenate([wk_ref[:, 128:], wo[:, 128:]], axis=1)


def spread(into, value, odd):
    zero = jnp.zeros_like(value)
    into[PATCHES:BLOCK] = zero[: BLOCK - PATCHES]
    end = HALF_AT + HALF_FIRST + HALF
    into[end:] = zero[: ROWS - end]

    @pl.when(odd == 0)
    def _():
        into[:PATCHES] = value[:PATCHES]
        into[BLOCK:end] = value[PATCHES:]

    @pl.when(odd == 1)
    def _():
        into[:PATCHES] = value[HALF : HALF + PATCHES]
        into[BLOCK : BLOCK + PATCHES] = value[HALF + PATCHES :]
        into[BLOCK + PATCHES : end] = value[:HALF]


def gather_back(into, value, odd):
    end = HALF_AT + HALF_FIRST + HALF

    @pl.when(odd == 0)
    def _():
        into[:PATCHES] = value[:PATCHES]
        into[PATCHES:] = value[BLOCK:end]

    @pl.when(odd == 1)
    def _():
        into[:HALF] = value[BLOCK + PATCHES : end]
        into[HALF : HALF + PATCHES] = value[:PATCHES]
        into[HALF + PATCHES :] = value[BLOCK : BLOCK + PATCHES]


def prep_kernel(info_ref, x_ref, c_ref, xo_ref, vec_ref, xp_ref, cp_ref, cb_ref, h_ref, other):
    odd = info_ref[ODD]
    gain, shift = vec_ref[0:1, :], vec_ref[1:2, :]
    spread(xp_ref, x_ref[...].astype(F32), odd)
    spread(cp_ref, c_ref[...], odd)
    cb_ref[...] = cp_ref[...].astype(BF)
    normed, _ = ln_stats(xp_ref[...])
    h_ref[:ROWS] = (normed * gain + shift).astype(BF)
    other[...] = jnp.zeros_like(other)
    other[HALF_FIRST : HALF_FIRST + HALF] = xo_ref[...].astype(F32)
    normed, _ = ln_stats(other[...])
    h_ref[ROWS:] = (normed * gain + shift).astype(BF)


def forward_kernel(pieces, info_ref, h_ref, x_ref, vec_ref, *refs):
    sources, refs = refs[:pieces], refs[pieces:]
    qkv_ref, o_ref, a_ref, y_ref, h2_ref, w, sem = refs
    n = pl.program_id(0)
    bring(info_ref, sources, w, sem, 0, PANELS)
    a_ref[0] = w[n]
    qkv_ref[0] = nn(h_ref[...], w[n]).astype(BF)
    valid = lanes_below((BLOCK, BLOCK), PATCHES)
    for at in FRAMES_AT:
        q01, k01, v01, qv2, ko2 = split(qkv_ref[0, at : at + BLOCK, :])
        o_ref[0, at : at + BLOCK, :] = attend((q01, qv2), (k01, v01, qv2, ko2), valid)
    q01, k01, v01, qv2, ko2 = split(qkv_ref[0, HALF_AT:, :])
    valid = half_place((HALF_ROWS, 2 * HALF_ROWS), 1)
    part = attend((q01[:HALF_ROWS], qv2[:HALF_ROWS]), (k01, v01, qv2, ko2), valid)
    first = lax.broadcasted_iota(jnp.int32, (16, 256), 0) < HALF_FIRST
    o_ref[0, HALF_AT : HALF_AT + 16] = jnp.where(first, o_ref[0, HALF_AT : HALF_AT + 16], part[:16])
    o_ref[0, HALF_AT + 16 :] = part[16:]
    o = o_ref[0]
    z = nt(o[:, :128], a_ref[0, :, 384:512]) + nt(o[:, 128:], a_ref[0, :, 640:768])

    @pl.when(n == 0)
    def _():
        y_ref[...] = x_ref[...] + z

    @pl.when(n > 0)
    def _():
        y_ref[...] += z

    @pl.when(n == PANELS - 1)
    def _():
        normed, _ = ln_stats(y_ref[...])
        h2_ref[...] = (normed * vec_ref[2:3, :] + vec_ref[3:4, :]).astype(BF)


def store_blocks(out_ref, value, me, part=0):
    blocks = out_ref.shape[1]
    rows = value.shape[0] // blocks
    value = value.astype(BF)
    for w in range(blocks):
        if blocks == 1:
            place = 0
        else:
            r = jnp.bitwise_xor(w, me)
            place = (r & 2) * 2 + (r & 1) * 2 + lax.shift_right_logical(r, 2)
        out_ref[0, place, part * rows : (part + 1) * rows] = value[w * rows : (w + 1) * rows]


def mlp_kernel(last, info_ref, h_ref, cb_ref, b_ref, u_ref, d_ref, *refs):
    if last:
        base_ref, c_ref, y_ref, vec_ref, act_ref, dm_ref, db_ref, dy_ref, dz_ref, sums_ref, *refs = refs
        ht, ct, dub, acc = refs
    else:
        act_ref, dm_ref, db_ref, acc, ht, ct, dub = refs
    n = pl.program_id(0)

    @pl.when(n == 0)
    def _():
        ht[...] = h_ref[...].T
        ct[...] = cb_ref[...].T

    for j in range(3):
        cols = slice(256 * j, 256 * j + 256)
        up = u_ref[:, 0, 0, :, cols].reshape(D, 256)
        down = d_ref[:, 0, 0, :, cols].reshape(D, 256)
        u = nn(h_ref[...], up) + b_ref[0, :, cols]
        big = 0.5 * (1.0 + lax.erf(u * (0.5**0.5)))
        small = jnp.exp(-0.5 * u * u) * 0.3989422804014327
        act_ref[0, :, cols] = (u * big).astype(BF)
        du = nn(cb_ref[...], down) * (big + u * small)
        db_ref[0, :, cols] = jnp.sum(du, axis=0, keepdims=True)
        dub[:, cols] = du.astype(BF)
    dh = nt(dub[...], u_ref[...].reshape(D, D))
    store_blocks(dm_ref, nn(ht[...], dub[...]), info_ref[WIDE], 0)
    store_blocks(dm_ref, nn(ct[...], act_ref[0]), info_ref[WIDE], 1)

    @pl.when(n == 0)
    def _():
        acc[...] = base_ref[...] + dh if last else dh

    @pl.when(n == 1)
    def _():
        acc[...] += dh
        if last:
            normed, rstd = ln_stats(y_ref[...])
            grad = acc[...]
            c = c_ref[...]
            dy = c + ln_back(grad, normed, rstd, vec_ref[2:3, :])
            dy_ref[...] = dy
            dz_ref[...] = dy.astype(BF)
            sums_ref[0:1, :] = jnp.sum(grad * normed, axis=0, keepdims=True)
            sums_ref[1:2, :] = jnp.sum(grad, axis=0, keepdims=True)
            sums_ref[2:3, :] = jnp.sum(c, axis=0, keepdims=True)


def back_kernel(info_ref, dz_ref, dzo_ref, h_ref, qkv_ref, o_ref, a_ref, dam_ref, dat0_ref, dat1_ref, dq_ref, ht, dt, dob):
    n = pl.program_id(0)

    @pl.when(n == 0)
    def _():
        ht[...] = h_ref[:ROWS].T
        dt[...] = dz_ref[...].T

    for into, cols in ((0, 384), (128, 640)):
        weight = a_ref[0, :, cols : cols + 128]
        dob[:ROWS, into : into + 128] = nn(dz_ref[...], weight).astype(BF)
        dob[ROWS:, into : into + 128] = nn(dzo_ref[...], weight).astype(BF)
    valid = lax.broadcasted_iota(jnp.int32, (BLOCK, BLOCK), 0) < PATCHES
    for at in FRAMES_AT:
        q01, k01, v01, qv2, ko2 = split(qkv_ref[0, at : at + BLOCK, :])
        d = dob[at : at + BLOCK]
        inside = lax.broadcasted_iota(jnp.int32, d.shape, 0) < PATCHES
        d = jnp.where(inside, d, jnp.zeros_like(d))
        dq_ref[0, at : at + BLOCK] = attend_back(
            (q01, qv2), (k01, v01, qv2, ko2), d, valid, BLOCK
        )
    q01, k01, v01, qv2, ko2 = split(qkv_ref[0, HALF_AT:, :])
    d = dob[HALF_AT:]
    d = jnp.where(half_place(d.shape, 0), d, jnp.zeros_like(d))
    valid = half_place((2 * HALF_ROWS, 2 * HALF_ROWS), 0)
    part = attend_back((q01, qv2), (k01, v01, qv2, ko2), d, valid, HALF_ROWS)
    first = lax.broadcasted_iota(jnp.int32, (16, D), 0) < HALF_FIRST
    dq_ref[0, HALF_AT : HALF_AT + 16] = jnp.where(first, dq_ref[0, HALF_AT : HALF_AT + 16], part[:16])
    dq_ref[0, HALF_AT + 16 :] = part[16:]
    left = nn(ht[...], dq_ref[0, :, 0:384])
    right = nn(ht[...], dq_ref[0, :, 512:768])
    outs = nn(dt[...], o_ref[0])
    value = jnp.concatenate(
        [left, outs[:, 0:128], right[:, 0:128], right[:, 128:256] + outs[:, 128:256]], axis=1
    )

    @pl.when(n < 2)
    def _():
        store_blocks(dam_ref, value, info_ref[WIDE])

    @pl.when(n == 2)
    def _():
        store_blocks(dat0_ref, value, info_ref[WIDE])

    @pl.when(n == 3)
    def _():
        store_blocks(dat1_ref, value, info_ref[WIDE])


def tokens_kernel(
    info_ref, dq_ref, a_ref, x_ref, dy_ref, vec_ref, sums_ref, dbm_ref, dbt_ref, grad_ref, small_ref, acc
):
    n = pl.program_id(0)
    dh = nt(dq_ref[0], a_ref[0])

    @pl.when(n == 0)
    def _():
        acc[...] = dh

    @pl.when(n > 0)
    def _():
        acc[...] += dh

    @pl.when(n == pl.num_programs(0) - 1)
    def _():
        normed, rstd = ln_stats(x_ref[...])
        grad = acc[...]
        small_ref[0:1, :] = jnp.sum(grad * normed, axis=0, keepdims=True)
        small_ref[1:2, :] = jnp.sum(grad, axis=0, keepdims=True)
        small_ref[2:5, :] = sums_ref[0:3, :]
        for j in range(PANELS):
            at = info_ref[BACK + j]

            @pl.when(at < 2)
            def _():
                small_ref[5 + j : 6 + j, :] = dbm_ref[at]

            @pl.when(at >= 2)
            def _():
                small_ref[5 + j : 6 + j, :] = dbt_ref[at - 2]

        gather_back(grad_ref, dy_ref[...] + ln_back(grad, normed, rstd, vec_ref[0:1, :]), info_ref[ODD])


def result_kernel(info_ref, actm_ref, actt_ref, d_ref, y_ref, vec_ref, out_ref, acc, left):
    n = pl.program_id(0)
    pick(actm_ref, actt_ref, left)
    y2 = nt(left[...], d_ref[...].reshape(D, D))

    @pl.when(n == 0)
    def _():
        acc[...] = y_ref[...] + y2 + vec_ref[4:5, :]

    @pl.when(n > 0)
    def _():
        acc[...] += y2

    @pl.when(n == pl.num_programs(0) - 1)
    def _():
        gather_back(out_ref, acc[...], info_ref[ODD])


WIDE, ODD, BACK, ORDER = 0, 1, 2, 6
PANELS = 4


def spec(shape, kind, start):
    tail = (0,) * (len(shape) - 1)
    block = (1,) + tuple(shape[1:])
    if kind == "any":
        return pl.BlockSpec(memory_space=pl.ANY)
    if kind == "fixed":
        return pl.BlockSpec(shape, lambda n, info: (0,) + tail)
    if kind == "panel":
        return pl.BlockSpec(block, lambda n, info: (n + start,) + tail)
    if kind == "local":
        return pl.BlockSpec(block, lambda n, info: (n,) + tail)
    if kind in ("up", "down"):
        which = int(kind == "down")
        block = (shape[0], 1, 1) + tuple(shape[3:])
        return pl.BlockSpec(block, lambda n, info: (0, info[ORDER + n + start], which, 0, 0))
    if kind == "mine":
        return pl.BlockSpec(block, lambda n, info: (jnp.minimum(n, 1),) + tail)
    return pl.BlockSpec(block, lambda n, info: (jnp.maximum(n - 2, 0),) + tail)


def call(kernel, info, ins, outs, scratch=(), units=0, steps=PANELS, start=0, vmem="back"):
    moved = sum(a.size * a.dtype.itemsize for a, _ in ins)
    return pl.pallas_call(
        kernel,
        grid_spec=pltpu.PrefetchScalarGridSpec(
            num_scalar_prefetch=1,
            grid=(steps,),
            in_specs=[spec(a.shape, k, start) for a, k in ins],
            out_specs=[spec(s, k, start) for s, _, k in outs],
            scratch_shapes=list(scratch),
        ),
        out_shape=[jax.ShapeDtypeStruct(s, d) for s, d, _ in outs],
        compiler_params=pltpu.CompilerParams(vmem_limit_bytes=VMEM[vmem] << 20),
        cost_estimate=pl.CostEstimate(
            flops=int(2 * ROWS * D * D * units * steps), bytes_accessed=int(moved * 2), transcendentals=0
        ),
    )(info, *[a for a, _ in ins])


CORE, LINE_Y, LINE_X, NEAR_Z, FAR_Z = 1, 2, 4, 8, 16


def make_swap(devices):
    def swap(value, bit):
        return lax.ppermute(value, ("wide", "narrow"), [(i, i ^ bit) for i in range(devices)])

    return swap


def after(value, *others):
    return lax.optimization_barrier((value,) + others)[0] if others else value


class Gather:
    def __init__(self, swap, own):
        self.swap, self.own = swap, own

    def far(self, *wait):
        own = after(self.own, *wait)
        self.b0 = jnp.stack([own, self.swap(own, FAR_Z)])

    def near(self, *wait):
        self.b1 = self.swap(after(self.b0, *wait), NEAR_Z)

    def planes0(self, *wait):
        b0 = after(self.b0, *wait)
        self.x0, self.y0 = self.swap(b0, LINE_X), self.swap(b0, LINE_Y)

    def planes1(self, *wait):
        b1 = after(self.b1, *wait)
        self.x1, self.y1 = self.swap(b1, LINE_X), self.swap(b1, LINE_Y)

    def corners(self, *wait):
        x0, y1 = after(self.x0, *wait), after(self.y1, *wait)
        self.d0, self.d1 = self.swap(x0, LINE_Y), self.swap(y1, LINE_X)

    def mine(self):
        return [self.b0, self.b1, self.x0, self.x1, self.y0, self.y1, self.d0, self.d1]

    def theirs(self):
        return [self.swap(v, CORE) for v in self.mine()]


def merge_kernel(own_ref, *refs):
    got_refs, (keep_a, send_a, keep_b, send_b) = refs[:-4], refs[-4:]
    y, k = pl.program_id(0), pl.program_id(1)
    got = got_refs[0][...]
    if len(got_refs) == 2:
        got = jnp.where(y == 0, got, got_refs[1][...])
    value = (own_ref[...].astype(F32) + got.astype(F32)).astype(BF)

    @pl.when(k == 0)
    def _():
        keep_a[...] = value

    @pl.when(k == 1)
    def _():
        send_a[...] = value

    @pl.when((k >= 2) & (y == 0))
    def _():
        keep_b[...] = value

    @pl.when((k >= 2) & (y == 1))
    def _():
        send_b[...] = value


def merge(own, *got):
    rows = own.shape[2]
    block = (1, 2, rows, D)
    taken = pl.BlockSpec(block, lambda y, k: (y, k, 0, 0))
    by_y = pl.BlockSpec(block, lambda y, k: (y, 0, 0, 0))
    first = pl.BlockSpec(block, lambda y, k: (jnp.where(y == 0, jnp.maximum(k - 2, 0), 1), 0, 0, 0))
    second = pl.BlockSpec(block, lambda y, k: (jnp.where(y == 0, 0, jnp.maximum(k - 2, 0)), 0, 0, 0))
    size = own.size * 2
    gots = [taken]
    if len(got) == 2:
        gots = [
            pl.BlockSpec(block, lambda y, k: (0, jnp.where(y == 0, k, 3), 0, 0)),
            pl.BlockSpec(block, lambda y, k: (0, jnp.where(y == 0, 0, k), 0, 0)),
        ]
    return pl.pallas_call(
        merge_kernel,
        grid=(2, 4),
        in_specs=[taken] + gots,
        out_specs=[by_y, by_y, first, second],
        out_shape=[jax.ShapeDtypeStruct((2, 2, rows, D), BF)] * 4,
        compiler_params=pltpu.CompilerParams(vmem_limit_bytes=VMEM["merge"] << 20),
        cost_estimate=pl.CostEstimate(flops=0, bytes_accessed=3 * size, transcendentals=0),
    )(own, *got)


def total(*parts):
    value = parts[0].astype(F32)
    for p in parts[1:]:
        value = value + p.astype(F32)
    return value


class Scatter:
    def __init__(self, swap, *other):
        self.swap, self.state = swap, 0
        self.flight = tuple(swap(v, CORE) for v in other)

    def step(self, *wait, own=None):
        swap = self.swap
        got = lax.optimization_barrier(self.flight + wait)[: len(self.flight)]
        self.state += 1
        if self.state == 1:
            self.a, send_a, self.b, send_b = merge(own, *got)
            self.flight = swap(send_a, LINE_X), swap(send_b, LINE_Y)
            return (send_a, send_b)
        if self.state == 2:
            send_a = total(self.a[1], got[0][1]).astype(BF)
            send_b = total(self.b[1], got[1][1]).astype(BF)
            self.a, self.b = (self.a[0], got[0][0]), (self.b[0], got[1][0])
            self.flight = swap(send_a, LINE_Y), swap(send_b, LINE_X)
            return (send_a, send_b)
        if self.state == 3:
            self.a = self.a + (got[0],)
            send = total(*self.b, got[1]).astype(BF)
            self.flight = (swap(send, NEAR_Z),)
            return (send,)
        if self.state == 4:
            self.a = self.a + (got[0],)
            send = total(*(p[1] for p in self.a)).astype(BF)
            self.flight = (swap(send, FAR_Z),)
            return (send,)
        self.result = total(*(p[0] for p in self.a), got[0])
        return (self.result,)


def body(
    tokens_in,
    cotangent,
    norm1_gain,
    norm1_shift,
    w_query,
    w_key,
    w_value,
    w_out,
    norm2_gain,
    norm2_shift,
    w_up,
    up_bias,
    w_down,
    down_bias,
    *,
    wide,
    narrow,
):
    direct = wide == 8 and narrow == 4
    wi, ni = lax.axis_index("wide"), lax.axis_index("narrow")
    swap = make_swap(wide * narrow)
    flipped = jnp.array([0, 2, 1, 3], jnp.int32)
    places = jnp.arange(PANELS, dtype=jnp.int32)
    back = flipped[jnp.bitwise_xor(ni, places)] if direct else places
    order = jnp.bitwise_xor(ni, flipped) if direct else places
    me = wi if direct else jnp.zeros_like(wi)
    info = jnp.concatenate(
        [v.astype(jnp.int32) for v in (me.reshape(1), (ni % 2).reshape(1), back, order)]
    )
    count, rows = tokens_in.shape[0], w_up.shape[0]
    vecs = jnp.stack([norm1_gain, norm1_shift, norm2_gain, norm2_shift, down_bias] + [down_bias] * 3)
    wide_row, turned = pltpu.VMEM((ROWS, D), F32), pltpu.VMEM((D, ROWS), BF)
    tokens32, tokens16 = ((ROWS, D), F32, "fixed"), ((ROWS, D), BF, "fixed")
    result32 = ((count, D), F32, "fixed")
    sums = ((8, D), F32, "fixed")
    blocks = 8 if direct else 1
    grads_a, grads_m = (2, blocks, D // blocks, D), (2, blocks, 2 * D // blocks, D)

    mlp = jnp.concatenate([w_up, w_down.T])
    if direct:
        full = lax.all_gather(mlp, ("wide", "narrow"), axis=0, tiled=False)
        full = full.reshape(wide, narrow, 2, rows, D)
    (attn,) = pl.pallas_call(
        pack_kernel,
        out_shape=[jax.ShapeDtypeStruct((rows, D), BF)],
        compiler_params=pltpu.CompilerParams(vmem_limit_bytes=VMEM["pack"] << 20),
    )(w_query, w_key, w_value, w_out)
    shared = jnp.where(ni % 2 == 1, tokens_in[:HALF], tokens_in[count - HALF :])
    shared = swap(shared, CORE)
    x, c, cb, h1 = call(
        prep_kernel,
        info,
        [(tokens_in, "fixed"), (cotangent, "fixed"), (shared, "fixed"), (vecs, "fixed")],
        [tokens32, tokens32, tokens16, ((ROWS + HALF_ROWS, D), BF, "fixed")],
        [pltpu.VMEM((HALF_ROWS, D), F32)],
        steps=1,
        vmem="prep",
    )
    if direct:
        ga = Gather(swap, attn)
        ga.far()
        ga.near()
        ga.planes0()
        ga.planes1(h1)
        ga.corners()
        sources = ga.mine() + ga.theirs()
        b_y, b_c = swap(after(up_bias, ga.d0, ga.d1), LINE_Y), swap(up_bias, CORE)
    else:

        def whole(v):
            return lax.all_gather(v, "narrow", axis=0, tiled=False)

        sources = [whole(lax.all_gather(attn, "wide", axis=0, tiled=True))]
        full = lax.all_gather(mlp.reshape(2, rows, D), "wide", axis=1, tiled=True)
        full = whole(full)[None]
        biases = whole(up_bias)
    qkv, o, a, y, h2 = call(
        functools.partial(forward_kernel, len(sources)),
        info,
        [(h1, "fixed"), (x, "fixed"), (vecs, "fixed")] + [(v, "any") for v in sources],
        [((PANELS, ROWS + HALF_ROWS, D), BF, "panel"), ((PANELS, ROWS, 256), BF, "panel")]
        + [((PANELS, D, D), BF, "panel"), tokens32, tokens16],
        [pltpu.VMEM((PANELS, D, D), BF), pltpu.SemaphoreType.DMA((PANELS, 8))],
        units=2,
        vmem="forward",
    )

    if direct:
        b_y = after(b_y, h2)
        biases = jnp.stack([up_bias, b_y, b_c, swap(b_y, CORE)])
    biases = biases.reshape(PANELS, 1, D)

    def mlp_part(start, more_in, more_out, more_scratch):
        return call(
            functools.partial(mlp_kernel, not start),
            info,
            [(h2, "fixed"), (cb, "fixed"), (biases, "panel"), (full, "up"), (full, "down")] + more_in,
            [((2, ROWS, D), BF, "local"), (grads_m, BF, "local"), ((2, 1, D), F32, "local")] + more_out,
            [turned, turned, pltpu.VMEM((ROWS, D), BF)] + more_scratch,
            units=5,
            steps=2,
            start=start,
            vmem="mlp",
        )

    act_t, dm_t, db_t, acc = mlp_part(2, [], [tokens32], [])
    if direct:
        sm = Scatter(swap, dm_t)
    act_m, dm_m, db_m, dy, dz, sums2 = mlp_part(
        0,
        [(acc, "fixed"), (c, "fixed"), (y, "fixed"), (vecs, "fixed")],
        [tokens32, tokens16, sums],
        [wide_row],
    )
    dzo = swap(dz[HALF_AT:], CORE)
    if direct:
        dz = after(dz, *sm.step(dz, own=dm_m))

    grads_one = ((1,) + grads_a[1:], BF, "fixed")
    da_m, *da_t, dq = call(
        back_kernel,
        info,
        [(dz, "fixed"), (dzo, "fixed"), (h1, "fixed"), (qkv, "panel"), (o, "panel"), (a, "panel")],
        [(grads_a, BF, "mine"), grads_one, grads_one, ((PANELS, ROWS, D), BF, "panel")],
        [turned, turned, pltpu.VMEM((ROWS + HALF_ROWS, 256), BF)],
        units=4,
    )
    grad_x, small = call(
        tokens_kernel,
        info,
        [(dq, "panel"), (a, "panel"), (x, "fixed"), (dy, "fixed"), (vecs, "fixed"), (sums2, "fixed")]
        + [(db_m, "fixed"), (db_t, "fixed")],
        [result32, ((16, D), F32, "fixed")],
        [wide_row],
        units=1,
        vmem="late",
    )
    if direct:
        sa = Scatter(swap, *da_t)
        sent = sm.step(small)
        act_m = after(act_m, *sent, *sa.step(*sent, own=da_m))
    (out,) = call(
        result_kernel,
        info,
        [(act_m, "mine"), (act_t, "theirs"), (full, "down"), (y, "fixed"), (vecs, "fixed")],
        [result32],
        [wide_row, pltpu.VMEM((ROWS, D), BF)],
        units=1,
        vmem="late",
    )
    if direct:

        def reduced(small, bit, *wait):
            small = after(small, *wait)
            return small + swap(small, bit)

        near = sm.step(out)
        small = reduced(reduced(small, CORE), LINE_X, *near)
        small = reduced(small, FAR_Z, *sa.step(small))
        far = sm.step()
        small = reduced(small, NEAR_Z, *sa.step(small, *far))
        small = reduced(small, LINE_Y, *sa.step(small, *sm.step()))
        sa.step()
        grad_a, grad_u, grad_d = sa.result, sm.result[:rows], sm.result[rows:]
    else:

        def shard(own, other):
            v = jnp.concatenate([own, other]).reshape(PANELS, -1, D, D).astype(F32)
            v = lax.psum_scatter(v, "narrow", scatter_dimension=0, tiled=False)
            return lax.psum_scatter(v, "wide", scatter_dimension=1, tiled=True)

        (grad_a,), (grad_u, grad_d) = shard(da_m, jnp.concatenate(da_t)), shard(dm_m, dm_t)
        small = lax.psum(small, ("wide", "narrow"))
    pick_lanes = lambda low, high: jnp.concatenate(
        [grad_a[:, low : low + 128], grad_a[:, high : high + 64]], axis=1
    )
    return (
        out,
        grad_x,
        small[0],
        small[1],
        pick_lanes(0, 512),
        pick_lanes(128, 640),
        pick_lanes(256, 576),
        pick_lanes(384, 704).T,
        small[2],
        small[3],
        grad_u,
        lax.dynamic_index_in_dim(small, 5 + ni, 0, keepdims=False),
        grad_d.T,
        small[4],
    )


def solution(mesh):
    rows, cols, copied = P("wide", "narrow"), P("narrow", "wide"), P()
    tokens = P(("wide", "narrow"), None)
    return jax.shard_map(
        functools.partial(body, wide=mesh.shape["wide"], narrow=mesh.shape["narrow"]),
        mesh=mesh,
        in_specs=(tokens, tokens, copied, copied, rows, rows, rows, cols)
        + (copied, copied, rows, P("narrow"), cols, copied),
        out_specs=(tokens, tokens, copied, copied, rows, rows, rows, cols)
        + (copied, copied, rows, P("narrow"), cols, copied),
        check_vma=False,
    )
```
